32 devices in a mesh: row: 8 (over z, y), col: 4 (over x, core).
Axes of the slice: x: 2, y: 2, z: 4, core: 2. Of those that a mesh axis runs over, the one named last changes fastest.
Arguments:
- patches: bfloat16 [64, 64, 384], P('row', 'col'), may hold values from -10 to 10
- tissue: int32 [64, 64], P('row', 'col'), may hold values from 0 to 1
- in_weight: bfloat16 [384, 1536], replicated, may hold values from -0.3125 to 0.3125
- conv_weight: float32 [3, 3, 768], replicated, may hold values from -2 to 2
- conv_bias: float32 [768], replicated, may hold values from -3 to 3
- x_weight: bfloat16 [768, 224], replicated, may hold values from -0.21875 to 0.21875
- dt_weight: bfloat16 [4, 24, 768], replicated, may hold values from -1.25 to 1.25
- dt_bias: float32 [4, 768], replicated, may hold values from -5.5 to -3.5
- decay_rate: float32 [4, 768, 16], replicated, may hold values from 0.0001 to 4
- skip_gain: float32 [768], replicated, may hold values from 0.5 to 2
- norm_gain: float32 [768], replicated, may hold values from 0.1 to 1.9
- out_weight: bfloat16 [768, 384], replicated, may hold values from -0.21875 to 0.21875
Outputs:
- result: bfloat16 [64, 64, 384], P('row', 'col')
The draws below stay inside these ranges and needn't reach their ends.
All inputs are finite; a program needn't handle non-finite values.
Results may differ from the reference program's by a relative error of at most 0.0076.
Values may be sent and summed in bfloat16 or wider, within the bound.
A program may use at most 256 MiB of HBM per device.

```python
import math
import jax
import jax.numpy as jnp
from jax import lax

CH = 384
INNER = 768
STATE = 16
RANK = 24
IMG_H = 64
IMG_W = 64


def draw_patches(key, part):
    base_key = jax.random.fold_in(key, 101)
    key_noise, key_rows, key_cols = jax.random.split(base_key, 3)
    noise_part = jnp.clip(jax.random.normal(key_noise, (IMG_H, IMG_W, CH), jnp.float32), -4.0, 4.0)
    spread = math.log(2.0)
    row_scale = jnp.exp(jax.random.uniform(key_rows, (IMG_H, 1, 1), jnp.float32, -spread, spread))
    col_scale = jnp.exp(jax.random.uniform(key_cols, (1, IMG_W, 1), jnp.float32, -spread, spread))
    values = noise_part * row_scale * col_scale
    return jnp.clip(values, -10.0, 10.0).astype(jnp.bfloat16)


def draw_tissue(key, part):
    base_key = jax.random.fold_in(key, 202)
    key_rows, key_cols, key_cells = jax.random.split(base_key, 3)
    row_live = jax.random.randint(key_rows, (IMG_H, 1), 0, 4) > 0
    col_live = jax.random.randint(key_cols, (1, IMG_W), 0, 4) > 0
    cell_live = jax.random.randint(key_cells, (IMG_H, IMG_W), 0, 8) > 0
    return jnp.logical_and(jnp.logical_and(row_live, col_live), cell_live).astype(jnp.int32)


def bell_draw(stream_key, dims, deviation, most, held_as=jnp.bfloat16):
    drawn = jax.random.normal(stream_key, dims, jnp.float32) * deviation
    return jnp.minimum(jnp.maximum(drawn, -most), most).astype(held_as)


def setup_inputs(seed: int = 0) -> dict:
    arg_keys = jax.random.split(jax.random.key(seed), 13)
    patches = draw_patches(jax.random.fold_in(arg_keys[12], 71), 0)
    tissue = draw_tissue(jax.random.fold_in(arg_keys[12], 71), 0)
    in_weight = bell_draw(arg_keys[2], (CH, 2 * INNER), CH ** -0.5, 0.3125)
    conv_weight = bell_draw(arg_keys[3], (3, 3, INNER), 9 ** -0.5, 2.0, jnp.float32)
    conv_bias = bell_draw(arg_keys[4], (INNER,), 0.5, 3.0, jnp.float32)
    x_weight = bell_draw(arg_keys[5], (INNER, 4 * (RANK + 2 * STATE)), INNER ** -0.5, 0.21875)
    dt_weight = bell_draw(arg_keys[6], (4, RANK, INNER), RANK ** -0.5, 1.25)
    dt_bias = jnp.clip(jax.random.uniform(arg_keys[7], (4, INNER), jnp.float32, -5.5, -3.5), -5.5, -3.5)
    decay_rate = jnp.clip(jnp.exp(jax.random.uniform(arg_keys[8], (4, INNER, STATE), jnp.float32, math.log(0.0001), math.log(4.0))), 0.0001, 4.0)
    skip_gain = jnp.clip(jax.random.uniform(arg_keys[9], (INNER,), jnp.float32, 0.5, 2.0), 0.5, 2.0)
    norm_gain = jnp.clip(1.0 + 0.18 * jax.random.normal(arg_keys[10], (INNER,), jnp.float32), 0.1, 1.9)
    out_weight = bell_draw(arg_keys[11], (INNER, CH), INNER ** -0.5, 0.21875)
    return dict(patches=patches, tissue=tissue, in_weight=in_weight, conv_weight=conv_weight, conv_bias=conv_bias, x_weight=x_weight, dt_weight=dt_weight, dt_bias=dt_bias, decay_rate=decay_rate, skip_gain=skip_gain, norm_gain=norm_gain, out_weight=out_weight)


def to_order(values, columns_first, backward):
    grid = values.reshape(IMG_H, IMG_W, -1)
    if columns_first:
        grid = jnp.transpose(grid, (1, 0, 2))
    series = grid.reshape(IMG_H * IMG_W, -1)
    if backward:
        series = series[::-1]
    return series

def from_order(series, columns_first, backward):
    if backward:
        series = series[::-1]
    if columns_first:
        grid = jnp.transpose(series.reshape(IMG_W, IMG_H, -1), (1, 0, 2))
    else:
        grid = series.reshape(IMG_H, IMG_W, -1)
    return grid.reshape(IMG_H * IMG_W, -1)

def selective(steps_dt, inputs_du, b_coeffs, c_coeffs, decays):

    def advance(carried, inputs):
        delta, driven, b_row, c_row = inputs
        carried = jnp.exp(-decays * delta[:, None]) * carried + driven[:, None] * b_row[None, :]
        return (carried, lax.optimization_barrier(jnp.sum(carried * c_row[None, :], axis=1)))
    start = jnp.zeros((INNER, STATE), jnp.float32)
    final_state, outputs = lax.scan(advance, start, (steps_dt, inputs_du, b_coeffs, c_coeffs))
    return outputs

def reference(patches, tissue, in_weight, conv_weight, conv_bias, x_weight, dt_weight, dt_bias, decay_rate, skip_gain, norm_gain, out_weight):
    token_count = IMG_H * IMG_W
    flattened = patches.reshape(token_count, CH)
    projected = jnp.dot(flattened, in_weight, preferred_element_type=jnp.float32)
    x_inner = projected[:, :INNER].astype(jnp.bfloat16).reshape(IMG_H, IMG_W, INNER)
    gate_half = projected[:, INNER:].astype(jnp.bfloat16)
    framed = jnp.pad(x_inner.astype(jnp.float32), ((1, 1), (1, 1), (0, 0)))
    conv_sum = jnp.zeros((IMG_H, IMG_W, INNER), jnp.float32) + conv_bias
    for offset_row in range(3):
        for offset_col in range(3):
            conv_sum = conv_sum + framed[offset_row:offset_row + IMG_H, offset_col:offset_col + IMG_W] * conv_weight[offset_row, offset_col]
    activated = jax.nn.silu(conv_sum).astype(jnp.bfloat16).reshape(token_count, INNER)
    scan_proj = jnp.dot(activated, x_weight, preferred_element_type=jnp.float32)
    tissue_live = tissue.reshape(token_count, 1).astype(jnp.float32)
    activated_wide = activated.astype(jnp.float32)
    width_each = RANK + 2 * STATE
    combined = jnp.zeros((token_count, INNER), jnp.float32)
    for direction in range(4):
        section = scan_proj[:, direction * width_each:(direction + 1) * width_each]
        low_rank = section[:, :RANK].astype(jnp.bfloat16)
        steps_dt = jax.nn.softplus(jnp.dot(low_rank, dt_weight[direction], preferred_element_type=jnp.float32) + dt_bias[direction]) * tissue_live
        inputs_du = steps_dt * activated_wide
        b_coeffs = section[:, RANK:RANK + STATE]
        c_coeffs = section[:, RANK + STATE:]
        columns_first = direction >= 2
        backward = direction % 2 == 1
        ordered = [to_order(member, columns_first, backward) for member in (steps_dt, inputs_du, b_coeffs, c_coeffs)]
        outputs = selective(ordered[0], ordered[1], ordered[2], ordered[3], decay_rate[direction])
        combined = combined + from_order(outputs, columns_first, backward)
    combined = combined + skip_gain * activated_wide
    mean_value = lax.optimization_barrier(jnp.mean(combined, axis=1, keepdims=True))
    centered = combined - mean_value
    variance = lax.optimization_barrier(jnp.mean(centered * centered, axis=1, keepdims=True))
    normed = centered * lax.rsqrt(variance + 1e-05) * norm_gain
    mixed = (normed * jax.nn.silu(gate_half.astype(jnp.float32))).astype(jnp.bfloat16)
    result = jnp.dot(mixed, out_weight, preferred_element_type=jnp.float32) * tissue_live
    return result.astype(jnp.bfloat16).reshape(IMG_H, IMG_W, CH)
```

```python
import functools
import math
import jax
import jax.numpy as jnp
from jax import lax
from jax.experimental import pallas as pl
from jax.experimental.pallas import tpu as pltpu
from jax.sharding import PartitionSpec as P

MESH = pl.DeviceIdType.MESH
VMEM = pl.BlockSpec(memory_space=pltpu.VMEM)
ANY = pl.BlockSpec(memory_space=pl.ANY)
LIMIT = 56 * 1024 * 1024
LOG2E = math.log2(math.e)
AROUND = ((-1, 0), (1, 0), (0, -1), (0, 1), (-1, -1), (-1, 1), (1, -1), (1, 1))


def lanes(width):
    return -(-width // 128) * 128


def halo_kernel(nr, nc, strips, out, send, recv):
    r, c = lax.axis_index("row"), lax.axis_index("col")
    peers = [(lax.rem(r + dr + nr, nr), lax.rem(c + dc + nc, nc)) for dr, dc in AROUND]
    barrier = pltpu.get_barrier_semaphore()
    for peer in peers:
        pl.semaphore_signal(barrier, inc=1, device_id=peer, device_id_type=MESH)
    pl.semaphore_wait(barrier, len(peers))
    copies = []
    for d, peer in enumerate(peers):
        copy = pltpu.make_async_remote_copy(
            src_ref=strips.at[d], dst_ref=out.at[d], send_sem=send.at[d], recv_sem=recv.at[d],
            device_id=peer, device_id_type=MESH)
        copy.start()
        copies.append(copy)
    for copy in copies:
        copy.wait()


def halo(strips, nr, nc):
    return pl.pallas_call(
        functools.partial(halo_kernel, nr, nc),
        out_shape=jax.ShapeDtypeStruct(strips.shape, strips.dtype),
        in_specs=[VMEM], out_specs=VMEM,
        scratch_shapes=[pltpu.SemaphoreType.DMA((8,)), pltpu.SemaphoreType.DMA((8,))],
        compiler_params=pltpu.CompilerParams(collective_id=0, has_side_effects=True),
        name="halo",
    )(strips)


def greet(sizes):
    barrier = pltpu.get_barrier_semaphore()
    for axis, n in sizes:
        me = lax.axis_index(axis)
        for k in range(1, n):
            pl.semaphore_signal(barrier, inc=1, device_id={axis: lax.rem(me + k, n)},
                                device_id_type=MESH)
    pl.semaphore_wait(barrier, sum(n - 1 for axis, n in sizes))


def swap_kernel(sizes, *refs):
    count = len(sizes)
    ins, outs, sems = refs[:count], refs[count:2 * count], refs[2 * count:]
    greet(sizes)
    copies = []
    for place, (axis, n) in enumerate(sizes):
        send, recv, own = sems[3 * place:3 * place + 3]
        me = lax.axis_index(axis)
        for k in range(1, n):
            to = lax.rem(me + k, n)
            copies.append(pltpu.make_async_remote_copy(
                src_ref=ins[place].at[to], dst_ref=outs[place].at[me],
                send_sem=send.at[k], recv_sem=recv.at[k],
                device_id={axis: to}, device_id_type=MESH))
        copies.append(pltpu.make_async_copy(ins[place].at[me], outs[place].at[me], own.at[0]))
    for copy in copies:
        copy.start()
    for copy in copies:
        copy.wait()


def swap(sizes, arrays, collective_id):
    scratch = []
    for axis, n in sizes:
        scratch += [pltpu.SemaphoreType.DMA((n,)), pltpu.SemaphoreType.DMA((n,)),
                    pltpu.SemaphoreType.DMA((1,))]
    return pl.pallas_call(
        functools.partial(swap_kernel, sizes),
        out_shape=[jax.ShapeDtypeStruct(a.shape, a.dtype) for a in arrays],
        in_specs=[ANY] * len(arrays), out_specs=[ANY] * len(arrays),
        scratch_shapes=scratch,
        compiler_params=pltpu.CompilerParams(collective_id=collective_id, has_side_effects=True),
        name="swap%d" % collective_id,
    )(*arrays)


def turn(rows, cols):
    count = rows * cols
    out = lax.broadcasted_iota(jnp.int32, (count, count), 0)
    src = lax.broadcasted_iota(jnp.int32, (count, count), 1)
    return (lax.rem(out, rows) * cols + lax.div(out, rows) == src).astype(jnp.float32).astype(jnp.bfloat16)


def turn_back(rows, cols):
    count = rows * cols
    out = lax.broadcasted_iota(jnp.int32, (count, count), 0)
    src = lax.broadcasted_iota(jnp.int32, (count, count), 1)
    return (lax.rem(out, cols) * rows + lax.div(out, cols) == src).astype(jnp.float32).astype(jnp.bfloat16)


def dot(a, b):
    return jnp.dot(a, b, preferred_element_type=jnp.float32)


def front_kernel(dims, patches, strips, live, w_in, w_conv, bias, w_x, tissue,
                 msg_row, msg_col, act_out, gate_out, frame):
    rows, cols, inner, nr, nc = dims
    tokens = rows * cols
    projected = dot(patches[...], w_in[...])
    gate_out[...] = projected[:, inner:].astype(jnp.bfloat16)
    body = projected[:, :inner].astype(jnp.bfloat16).astype(jnp.float32)
    rim = dot(strips[...], w_in[:, :inner]).astype(jnp.bfloat16).astype(jnp.float32) * live[...]
    frame[1:rows + 1, 1:cols + 1, :] = body.reshape(rows, cols, inner)
    frame[rows + 1, 1:cols + 1, :] = rim[0:cols]
    frame[0, 1:cols + 1, :] = rim[cols:2 * cols]
    for i in range(rows):
        frame[i + 1, cols + 1:cols + 2, :] = rim[2 * cols + i:2 * cols + i + 1]
        frame[i + 1, 0:1, :] = rim[3 * cols + i:3 * cols + i + 1]
    frame[rows + 1, cols + 1:cols + 2, :] = rim[4 * cols:4 * cols + 1]
    frame[rows + 1, 0:1, :] = rim[5 * cols:5 * cols + 1]
    frame[0, cols + 1:cols + 2, :] = rim[6 * cols:6 * cols + 1]
    frame[0, 0:1, :] = rim[7 * cols:7 * cols + 1]
    total = jnp.zeros((rows, cols, inner), jnp.float32) + bias[...]
    for r in range(3):
        for c in range(3):
            total = total + frame[r:r + rows, c:c + cols, :] * w_conv[3 * r + c:3 * r + c + 1, :]
    act = (total * jax.nn.sigmoid(total)).astype(jnp.bfloat16).reshape(tokens, inner)
    act_out[...] = act
    head = dot(act, w_x[...])
    mark = tissue[...].astype(jnp.float32)
    place = lax.broadcasted_iota(jnp.int32, (tokens, 128), 1)
    head_row = jnp.where(place == 112, mark, head[:, :128]).astype(jnp.bfloat16)
    head_col = jnp.where(place == 112, mark, head[:, 128:]).astype(jnp.bfloat16)
    flip = turn(rows, cols)
    head_row = dot(flip, head_row).astype(jnp.bfloat16)
    act_row = dot(flip, act).astype(jnp.bfloat16)
    for part, (msg, n, top, values) in enumerate(
            ((msg_row, nc, head_row, act_row), (msg_col, nr, head_col, act))):
        each = inner // n
        for g in range(n):
            msg[g, :, 0:128] = top
            msg[g, :, 128:128 + each] = values[:, g * each:(g + 1) * each]


def chain_pass(spec, refs, backward, states, outputs):
    chains, steps, width, state = spec
    dt_ref, du_ref, bc_ref, nd_ref, y_ref = refs
    b_at = 32 if backward else 0
    c_at = b_at + state
    col = width if backward else 0
    first = (not backward)

    def one(i, carry):
        held, total = carry
        t = steps - 1 - i if backward else i
        here = pl.ds(pl.multiple_of(t * chains, chains), chains)
        dt = dt_ref[here, col:col + width]
        du = du_ref[here, col:col + width]
        bc = bc_ref[here, :]
        y = None
        fresh = []
        for s in range(state):
            decay = jnp.exp2(nd_ref[s:s + 1, col:col + width] * dt)
            h = decay * held[s] + du * bc[:, b_at + s:b_at + s + 1]
            fresh.append(h)
            if outputs:
                term = h * bc[:, c_at + s:c_at + s + 1]
                y = term if y is None else y + term
        if outputs:
            if first:
                y_ref[here, :] = y
            else:
                y_ref[here, :] = y_ref[here, :] + y
            return tuple(fresh), total
        return tuple(fresh), total + dt

    return lax.fori_loop(0, steps, one, (states, jnp.zeros((chains, width), jnp.float32)), unroll=2)


def scan_kernel(specs, sizes, *refs):
    msgs, weights, biases, nds = refs[0:2], refs[2:4], refs[4:6], refs[6:8]
    ys = refs[8:10]
    scratch = refs[10:]
    greet(sizes)
    work = []
    for p in range(2):
        work.append(scratch[p * 10:(p + 1) * 10])
    for p, (chains, steps, width, each, state) in enumerate(specs):
        dt_s, du_s, bc_s, y_s, end_s, sum_s, slots, send, recv, entry_s = work[p]
        axis, n = sizes[p]
        block = 256

        def prepare(i, unused, p=p, width=width, each=each, dt_s=dt_s, du_s=du_s, bc_s=bc_s):
            here = pl.ds(pl.multiple_of(i * block, block), block)
            head = msgs[p][here, 0:128]
            wide = head.astype(jnp.float32)
            bc_s[here, :] = wide
            x = dot(head, weights[p][...]) + biases[p][...]
            dt = (jnp.maximum(x, 0.0) + jnp.log1p(jnp.exp(-jnp.abs(x)))) * wide[:, 112:113]
            dt_s[here, :] = dt
            act = msgs[p][here, 128:128 + width].astype(jnp.float32)
            if each < width:
                spot = lax.broadcasted_iota(jnp.int32, (block, width), 1)
                act = jnp.where(spot < each, act, 0.0)
            du_s[here, 0:width] = dt[:, 0:width] * act
            du_s[here, width:2 * width] = dt[:, width:2 * width] * act
            return unused

        lax.fori_loop(0, chains * steps // block, prepare, 0)
        me = lax.axis_index(axis)
        for b in range(2):
            col = b * width
            zero = tuple(jnp.zeros((chains, width), jnp.float32) for s in range(state))
            ends, total = chain_pass((chains, steps, width, state),
                                     (dt_s, du_s, bc_s, nds[p], y_s), b == 1, zero, False)
            for s in range(state):
                end_s[b, s] = ends[s]
            sum_s[b] = total
            nd = nds[p][:, col:col + width]
            held = jnp.zeros((state, width), jnp.float32)
            for r in (range(chains - 1, -1, -1) if b else range(chains)):
                held = jnp.exp2(nd * sum_s[b, r:r + 1, :]) * held + end_s[b, :, r, :]
            slots[me, b, 0:state, :] = held
            slots[me, b, state:state + 8, :] = jnp.broadcast_to(
                jnp.sum(total, axis=0, keepdims=True), (8, width))
        for k in range(1, n):
            to = lax.rem(me + k, n)
            pltpu.make_async_remote_copy(
                src_ref=slots.at[me], dst_ref=slots.at[me], send_sem=send.at[k],
                recv_sem=recv.at[k], device_id={axis: to}, device_id_type=MESH).start()
    for p, (chains, steps, width, each, state) in enumerate(specs):
        dt_s, du_s, bc_s, y_s, end_s, sum_s, slots, send, recv, entry_s = work[p]
        axis, n = sizes[p]
        me = lax.axis_index(axis)
        for k in range(1, n):
            to = lax.rem(me + k, n)
            source = lax.rem(me + n - k, n)
            pltpu.make_async_remote_copy(
                src_ref=slots.at[me], dst_ref=slots.at[me], send_sem=send.at[k],
                recv_sem=recv.at[k], device_id={axis: to}, device_id_type=MESH).wait_send()
            pltpu.make_async_remote_copy(
                src_ref=slots.at[source], dst_ref=slots.at[source], send_sem=send.at[k],
                recv_sem=recv.at[k], device_id={axis: to}, device_id_type=MESH).wait_recv()
        for b in range(2):
            col = b * width
            nd = nds[p][:, col:col + width]
            held = jnp.zeros((state, width), jnp.float32)
            for q in (range(n - 1, -1, -1) if b else range(n)):
                ahead = (q > me) if b else (q < me)
                keep = jnp.where(ahead, 1.0, 0.0)
                after = jnp.exp2(nd * slots[q, b, state:state + 1, :]) * held + slots[q, b, 0:state, :]
                held = held + keep * (after - held)
            for r in (range(chains - 1, -1, -1) if b else range(chains)):
                entry_s[:, r, :] = held
                held = jnp.exp2(nd * sum_s[b, r:r + 1, :]) * held + end_s[b, :, r, :]
            start = tuple(entry_s[s] for s in range(state))
            chain_pass((chains, steps, width, state),
                       (dt_s, du_s, bc_s, nds[p], y_s), b == 1, start, True)
        groups = ys[p].shape[0]
        count = chains * steps // groups
        for g in range(groups):
            ys[p][g] = y_s[g * count:(g + 1) * count, 0:each].astype(jnp.bfloat16)


def back_kernel(dims, y_row, y_col, act, gate, skip, gain, w_out, tissue, out, mixed):
    rows, cols, inner, nr, nc = dims
    flip = turn_back(rows, cols)
    each = inner // nc
    for g in range(nc):
        mixed[:, g * each:(g + 1) * each] = dot(flip, y_row[g])
    each = inner // nr
    for g in range(nr):
        here = slice(g * each, (g + 1) * each)
        mixed[:, here] = mixed[:, here] + y_col[g].astype(jnp.float32)
    total = mixed[...] + skip[...] * act[...].astype(jnp.float32)
    centered = total - jnp.mean(total, axis=1, keepdims=True)
    variance = jnp.mean(centered * centered, axis=1, keepdims=True)
    normed = centered * lax.rsqrt(variance + 1e-05) * gain[...]
    gate_wide = gate[...].astype(jnp.float32)
    value = (normed * (gate_wide * jax.nn.sigmoid(gate_wide))).astype(jnp.bfloat16)
    result = dot(value, w_out[...]) * tissue[...].astype(jnp.float32)
    out[...] = result.astype(jnp.bfloat16)


def local_call(kernel, shapes, arrays, scratch, name):
    return pl.pallas_call(
        kernel, out_shape=shapes, in_specs=[VMEM] * len(arrays),
        out_specs=jax.tree.map(lambda unused: VMEM, shapes), scratch_shapes=scratch,
        compiler_params=pltpu.CompilerParams(vmem_limit_bytes=LIMIT), name=name,
    )(*arrays)


def per_device(nr, nc, patches, tissue, in_weight, conv_weight, conv_bias, x_weight, dt_weight,
               dt_bias, decay_rate, skip_gain, norm_gain, out_weight):
    rows, cols, channels = patches.shape
    tokens = rows * cols
    inner = out_weight.shape[0]
    state = decay_rate.shape[2]
    rank = dt_weight.shape[1]
    wide = rank + 2 * state
    r, c = lax.axis_index("row"), lax.axis_index("col")
    bf, f32 = jnp.bfloat16, jnp.float32

    def strip(values):
        return jnp.pad(values, ((0, cols - values.shape[0]), (0, 0)))

    strips = jnp.stack([
        patches[0], patches[-1], strip(patches[:, 0]), strip(patches[:, -1]),
        strip(patches[0, :1]), strip(patches[0, -1:]), strip(patches[-1, :1]), strip(patches[-1, -1:]),
    ])
    got = halo(strips, nr, nc).reshape(8 * cols, channels)
    live = jnp.stack([
        ((r - dr >= 0) & (r - dr < nr) & (c - dc >= 0) & (c - dc < nc)) for dr, dc in AROUND])
    live = jnp.repeat(live.astype(f32), cols)[:, None]

    def heads(first):
        parts = []
        for o in (first, first + 1):
            base = o * wide
            parts.append(x_weight[:, base + rank:base + wide])
        for o in (first, first + 1):
            parts.append(x_weight[:, o * wide:o * wide + rank])
        joined = jnp.concatenate(parts, axis=1)
        return jnp.pad(joined, ((0, 0), (0, 128 - joined.shape[1])))

    w_x = jnp.concatenate([heads(0), heads(2)], axis=1)
    mark = tissue.reshape(tokens, 1)
    dims = (rows, cols, inner, nr, nc)
    each_row, each_col = inner // nc, inner // nr
    shapes = [
        jax.ShapeDtypeStruct((nc, tokens, 128 + lanes(each_row)), bf),
        jax.ShapeDtypeStruct((nr, tokens, 128 + lanes(each_col)), bf),
        jax.ShapeDtypeStruct((tokens, inner), bf),
        jax.ShapeDtypeStruct((tokens, inner), bf),
    ]
    msg_row, msg_col, act, gate = local_call(
        functools.partial(front_kernel, dims), shapes,
        (patches.reshape(tokens, channels), got, live, in_weight, conv_weight.reshape(9, inner),
         conv_bias[None], w_x, mark),
        [pltpu.VMEM((rows + 2, -(-(cols + 2) // 8) * 8, inner), f32)], "front")
    got_row, got_col = swap((("col", nc), ("row", nr)), (msg_row, msg_col), 1)

    def weights(first, place, each):
        width = lanes(each)
        picked = lax.dynamic_slice_in_dim(dt_weight[first:first + 2], place * each, each, 2)
        picked = jnp.pad(picked, ((0, 0), (0, 0), (0, width - each)))
        top = 4 * state
        w = jnp.concatenate([
            jnp.pad(picked[0], ((top, 128 - top - rank), (0, 0))),
            jnp.pad(picked[1], ((top + rank, 128 - top - 2 * rank), (0, 0)))], axis=1)
        bias = lax.dynamic_slice_in_dim(dt_bias[first:first + 2], place * each, each, 1)
        bias = jnp.pad(bias, ((0, 0), (0, width - each))).reshape(1, 2 * width)
        rate = lax.dynamic_slice_in_dim(decay_rate[first:first + 2], place * each, each, 1)
        rate = jnp.pad(jnp.transpose(rate, (2, 0, 1)) * -LOG2E, ((0, 0), (0, 0), (0, width - each)))
        return w, bias, rate.reshape(state, 2 * width)

    w_r, b_r, n_r = weights(0, c, each_row)
    w_c, b_c, n_c = weights(2, r, each_col)
    specs = ((rows, nc * cols, lanes(each_row), each_row, state),
             (cols, nr * rows, lanes(each_col), each_col, state))
    sizes = (("row", nr), ("col", nc))
    scratch = []
    for (chains, steps, width, each, unused), (axis, n) in zip(specs, sizes):
        count = chains * steps
        scratch += [
            pltpu.VMEM((count, 2 * width), f32), pltpu.VMEM((count, 2 * width), f32),
            pltpu.VMEM((count, 128), f32), pltpu.VMEM((count, width), f32),
            pltpu.VMEM((2, state, chains, width), f32), pltpu.VMEM((2, chains, width), f32),
            pltpu.VMEM((n, 2, state + 8, width), f32),
            pltpu.SemaphoreType.DMA((n,)), pltpu.SemaphoreType.DMA((n,)),
            pltpu.VMEM((state, chains, width), f32)]
    y_row, y_col = pl.pallas_call(
        functools.partial(scan_kernel, specs, sizes),
        out_shape=[jax.ShapeDtypeStruct((nc, tokens, each_row), bf),
                   jax.ShapeDtypeStruct((nr, tokens, each_col), bf)],
        in_specs=[VMEM] * 8, out_specs=[VMEM] * 2, scratch_shapes=scratch,
        compiler_params=pltpu.CompilerParams(
            collective_id=2, has_side_effects=True, vmem_limit_bytes=LIMIT),
        name="scan",
    )(got_row.reshape(nc * tokens, -1), got_col.reshape(nr * tokens, -1),
      w_r, w_c, b_r, b_c, n_r, n_c)
    y_row, y_col = swap((("col", nc), ("row", nr)), (y_row, y_col), 3)
    out = local_call(
        functools.partial(back_kernel, dims), jax.ShapeDtypeStruct((tokens, channels), bf),
        (y_row, y_col, act, gate, skip_gain[None], norm_gain[None], out_weight, mark),
        [pltpu.VMEM((tokens, inner), f32)], "back")
    return out.reshape(rows, cols, channels)


def solution(mesh):
    grid = P("row", "col")
    return jax.shard_map(
        functools.partial(per_device, mesh.shape["row"], mesh.shape["col"]), mesh=mesh,
        in_specs=(P("row", "col", None), grid) + (P(),) * 10,
        out_specs=P("row", "col", None), check_vma=False)
```

```python
import functools
import math
import jax
import jax.numpy as jnp
from jax import lax
from jax.experimental import pallas as pl
from jax.experimental.pallas import tpu as pltpu
from jax.sharding import PartitionSpec as P

MESH = pl.DeviceIdType.MESH
VMEM = pl.BlockSpec(memory_space=pltpu.VMEM)
LIMIT = 56 * 1024 * 1024
LOG2E = math.log2(math.e)
AROUND = ((-1, 0), (1, 0), (0, -1), (0, 1), (-1, -1), (-1, 1), (1, -1), (1, 1))


def lanes(width):
    return -(-width // 128) * 128


def greet(peers):
    barrier = pltpu.get_barrier_semaphore()
    for peer in peers:
        pl.semaphore_signal(barrier, inc=1, device_id=peer, device_id_type=MESH)
    pl.semaphore_wait(barrier, len(peers))


def swap(axis, n, src, dst, send, recv, own):
    me = lax.axis_index(axis)
    copies = []
    for k in range(1, n):
        to = lax.rem(me + k, n)
        copies.append(pltpu.make_async_remote_copy(
            src_ref=src.at[to], dst_ref=dst.at[me], send_sem=send.at[k], recv_sem=recv.at[k],
            device_id={axis: to}, device_id_type=MESH))
    copies.append(pltpu.make_async_copy(src.at[me], dst.at[me], own.at[0]))
    for copy in copies:
        copy.start()
    return copies


def finish(copies):
    for copy in copies:
        copy.wait()


def spread(axis, n, slots, send, recv):
    me = lax.axis_index(axis)
    copies = []
    for k in range(1, n):
        copies.append(pltpu.make_async_remote_copy(
            src_ref=slots.at[me], dst_ref=slots.at[me], send_sem=send.at[k], recv_sem=recv.at[k],
            device_id={axis: lax.rem(me + k, n)}, device_id_type=MESH))
    for copy in copies:
        copy.start()
    return copies


def one_hot(hits):
    return hits.astype(jnp.float32).astype(jnp.bfloat16)


def iota(shape, dim):
    return lax.broadcasted_iota(jnp.int32, shape, dim)


def turn(rows, cols):
    count = rows * cols
    out = lax.broadcasted_iota(jnp.int32, (count, count), 0)
    src = lax.broadcasted_iota(jnp.int32, (count, count), 1)
    return (lax.rem(out, rows) * cols + lax.div(out, rows) == src).astype(jnp.float32).astype(jnp.bfloat16)


def turn_back(rows, cols):
    count = rows * cols
    out = lax.broadcasted_iota(jnp.int32, (count, count), 0)
    src = lax.broadcasted_iota(jnp.int32, (count, count), 1)
    return (lax.rem(out, cols) * rows + lax.div(out, cols) == src).astype(jnp.float32).astype(jnp.bfloat16)


def dot(a, b):
    return jnp.dot(a, b, preferred_element_type=jnp.float32)


def rim_picks(rows, cols):
    shape = (8 * cols, rows * cols)
    out, src = iota(shape, 0), iota(shape, 1)
    d, k = lax.div(out, cols), lax.rem(out, cols)
    last = (rows - 1) * cols
    token = jnp.where(d == 0, k, last + k)
    token = jnp.where(d == 2, k * cols, token)
    token = jnp.where(d == 3, k * cols + cols - 1, token)
    token = jnp.where(d == 4, 0, token)
    token = jnp.where(d == 5, cols - 1, token)
    token = jnp.where(d == 6, last, token)
    token = jnp.where(d == 7, rows * cols - 1, token)
    return one_hot(token == src)


def head_picks(columns, rank, state):
    shape = (columns, 256)
    src, out = iota(shape, 0), iota(shape, 1)
    wide = rank + 2 * state
    part, m = lax.div(out, 128), lax.rem(out, 128)
    base = 2 * part * wide
    at = jnp.where(m < 2 * state, base + rank + m, base + wide + rank + m - 2 * state)
    at = jnp.where(m >= 4 * state, base + m - 4 * state, at)
    at = jnp.where(m >= 4 * state + rank, base + wide + m - 4 * state - rank, at)
    at = jnp.where(m >= 4 * state + 2 * rank, -1, at)
    return one_hot(at == src)


def tissue_column(tissue, rows, cols):
    count = rows * cols
    up = one_hot(lax.div(iota((count, rows), 0), cols) == iota((count, rows), 1))
    spread_out = dot(up, tissue[...].astype(jnp.float32).astype(jnp.bfloat16))
    mine = lax.rem(iota((count, cols), 0), cols) == iota((count, cols), 1)
    return jnp.sum(jnp.where(mine, spread_out, 0.0), axis=1, keepdims=True)


def front(dims, rim_copies, patches, rim_in, w_in, w_conv, extras, w_x, tissue,
          msg_row, msg_col, act_out, gate_out, frame):
    rows, cols, inner, nr, nc, rank, state = dims
    tokens = rows * cols
    projected = dot(patches[...], w_in[...])
    gate_out[...] = projected[:, inner:].astype(jnp.bfloat16)
    body = projected[:, :inner].astype(jnp.bfloat16).astype(jnp.float32)
    frame[1:rows + 1, 1:cols + 1, :] = body.reshape(rows, cols, inner)
    finish(rim_copies)
    rim = dot(rim_in[...].reshape(8 * cols, -1), w_in[:, :inner])
    rim = rim.astype(jnp.bfloat16).astype(jnp.float32)
    r, c = lax.axis_index("row"), lax.axis_index("col")
    pieces = []
    for d, (dr, dc) in enumerate(AROUND):
        inside = (r - dr >= 0) & (r - dr < nr) & (c - dc >= 0) & (c - dc < nc)
        pieces.append(rim[d * cols:(d + 1) * cols] * jnp.where(inside, 1.0, 0.0))
    frame[rows + 1, 1:cols + 1, :] = pieces[0]
    frame[0, 1:cols + 1, :] = pieces[1]
    for i in range(rows):
        frame[i + 1, cols + 1:cols + 2, :] = pieces[2][i:i + 1]
        frame[i + 1, 0:1, :] = pieces[3][i:i + 1]
    frame[rows + 1, cols + 1:cols + 2, :] = pieces[4][0:1]
    frame[rows + 1, 0:1, :] = pieces[5][0:1]
    frame[0, cols + 1:cols + 2, :] = pieces[6][0:1]
    frame[0, 0:1, :] = pieces[7][0:1]
    total = jnp.zeros((rows, cols, inner), jnp.float32) + extras[0:1, :]
    for i in range(3):
        for j in range(3):
            total = total + frame[i:i + rows, j:j + cols, :] * w_conv[i, j:j + 1, :]
    act = (total * jax.nn.sigmoid(total)).astype(jnp.bfloat16).reshape(tokens, inner)
    act_out[...] = act
    head = dot(act, w_x[...]).astype(jnp.bfloat16)
    head = dot(head, head_picks(w_x.shape[1], rank, state))
    mark = tissue_column(tissue, rows, cols)
    place = lax.rem(iota((tokens, 256), 1), 128)
    head = jnp.where(place == 4 * state + 2 * rank, mark, head).astype(jnp.bfloat16)
    flip = turn(rows, cols)
    head_row = dot(flip, head[:, :128]).astype(jnp.bfloat16)
    act_row = dot(flip, act).astype(jnp.bfloat16)
    for msg, n, top, values in ((msg_row, nc, head_row, act_row), (msg_col, nr, head[:, 128:], act)):
        each = inner // n
        for g in range(n):
            msg[g, :, 0:128] = top
            msg[g, :, 128:128 + each] = values[:, g * each:(g + 1) * each]


def gather_weights(first, place, each, width, rank, state, dt_weight, dt_bias, decay,
                   wd_s, bias_s, nd_s, ndb_s):
    inner = dt_weight.shape[2]
    shape = (inner, width)
    picks = (iota(shape, 0) == iota(shape, 1) + place * each) & (iota(shape, 1) < each)
    exact = picks.astype(jnp.float32)
    picks = exact.astype(jnp.bfloat16)
    top = 4 * state
    for b in range(2):
        here = slice(b * width, (b + 1) * width)
        w = dot(dt_weight[first + b], picks)
        above = top + b * rank
        w = jnp.concatenate([jnp.zeros((above, width), jnp.float32), w,
                             jnp.zeros((128 - above - rank, width), jnp.float32)], axis=0)
        wd_s[:, here] = w.astype(jnp.bfloat16)
        bias = jnp.broadcast_to(dt_bias[first + b:first + b + 1, :], (8, inner))
        bias_s[:, here] = jnp.dot(bias, exact, precision=lax.Precision.HIGHEST,
                                  preferred_element_type=jnp.float32)
        rate = jnp.dot(decay[first + b], exact, precision=lax.Precision.HIGHEST,
                       preferred_element_type=jnp.float32)
        rate = rate * -LOG2E
        nd_s[:, here] = rate
        for s in range(state):
            ndb_s[s, :, here] = jnp.broadcast_to(rate[s:s + 1], (8, width))


def chain_pass(spec, refs, backward, states, outputs):
    chains, steps, width, state = spec
    dt_ref, du_ref, bc_ref, ndb_ref, y_ref = refs
    b_at = 32 if backward else 0
    c_at = b_at + state
    col = width if backward else 0
    first = (not backward)

    def one(i, carry):
        held, total = carry
        t = steps - 1 - i if backward else i
        here = pl.ds(pl.multiple_of(t * chains, chains), chains)
        dt = dt_ref[here, col:col + width]
        du = du_ref[here, col:col + width]
        bc = bc_ref[here, :]
        y = None
        fresh = []
        for s in range(state):
            rate = ndb_ref[s, :, col:col + width]
            if chains > 8:
                rate = jnp.concatenate([rate] * (chains // 8), axis=0)
            decay = jnp.exp2(rate * dt)
            h = decay * held[s] + du * bc[:, b_at + s:b_at + s + 1]
            fresh.append(h)
            if outputs:
                term = h * bc[:, c_at + s:c_at + s + 1]
                y = term if y is None else y + term
        if outputs:
            if first:
                y_ref[here, :] = y
            else:
                y_ref[here, :] = y_ref[here, :] + y
            return tuple(fresh), total
        return tuple(fresh), total + dt

    return lax.fori_loop(0, steps, one, (states, jnp.zeros((chains, width), jnp.float32)), unroll=4)


def first_pass(spec, n, me, got, wd_s, bias_s, nd_s, ndb_s, dt_s, du_s, bc_s, y_s, end_s, sum_s, slots):
    chains, steps, width, each, rank, state = spec
    senders, block = got.shape[0], got.shape[1]
    mark_at = 4 * state + 2 * rank
    for g in range(senders):
        here = slice(g * block, (g + 1) * block)
        head = got[g, :, 0:128]
        wide = head.astype(jnp.float32)
        bc_s[here, :] = wide
        x = dot(head, wd_s[...]) + bias_s[0:1, :]
        dt = (jnp.maximum(x, 0.0) + jnp.log1p(jnp.exp(-jnp.abs(x)))) * wide[:, mark_at:mark_at + 1]
        dt_s[here, :] = dt
        act = got[g, :, 128:128 + width].astype(jnp.float32)
        if each < width:
            act = jnp.where(iota((block, width), 1) < each, act, 0.0)
        du_s[here, 0:width] = dt[:, 0:width] * act
        du_s[here, width:2 * width] = dt[:, width:2 * width] * act
    for b in range(2):
        col = b * width
        zero = tuple(jnp.zeros((chains, width), jnp.float32) for s in range(state))
        ends, total = chain_pass((chains, steps, width, state),
                                 (dt_s, du_s, bc_s, ndb_s, y_s), b == 1, zero, False)
        for s in range(state):
            end_s[b, s] = ends[s]
        sum_s[b] = total
        nd = nd_s[:, col:col + width]
        held = jnp.zeros((state, width), jnp.float32)
        for r in (range(chains - 1, -1, -1) if b else range(chains)):
            held = jnp.exp2(nd * sum_s[b, r:r + 1, :]) * held + end_s[b, :, r, :]
        slots[me, b, 0:state, :] = held
        slots[me, b, state:state + 8, :] = jnp.broadcast_to(
            jnp.sum(total, axis=0, keepdims=True), (8, width))


def second_pass(spec, n, me, nd_s, ndb_s, dt_s, du_s, bc_s, y_s, end_s, sum_s, slots, entry_s, y_out):
    chains, steps, width, each, rank, state = spec
    for b in range(2):
        col = b * width
        nd = nd_s[:, col:col + width]
        held = jnp.zeros((state, width), jnp.float32)
        for q in (range(n - 1, -1, -1) if b else range(n)):
            ahead = (q > me) if b else (q < me)
            keep = jnp.where(ahead, 1.0, 0.0)
            after = jnp.exp2(nd * slots[q, b, state:state + 1, :]) * held + slots[q, b, 0:state, :]
            held = held + keep * (after - held)
        for r in (range(chains - 1, -1, -1) if b else range(chains)):
            entry_s[:, r, :] = held
            held = jnp.exp2(nd * sum_s[b, r:r + 1, :]) * held + end_s[b, :, r, :]
        start = tuple(entry_s[s] for s in range(state))
        chain_pass((chains, steps, width, state),
                   (dt_s, du_s, bc_s, ndb_s, y_s), b == 1, start, True)
    groups, count = y_out.shape[0], y_out.shape[1]
    for g in range(groups):
        y_out[g] = y_s[g * count:(g + 1) * count, :].astype(jnp.bfloat16)


def kernel(dims, specs, patches, tissue, w_in, w_conv, extras, w_x, dt_weight, dt_bias, decay, w_out,
           out, picked, rim_in, frame, act, gate, mixed, rim_send, rim_recv, *scratch):
    rows, cols, inner, nr, nc, rank, state = dims
    r, c = lax.axis_index("row"), lax.axis_index("col")
    near = [(lax.rem(r + dr + nr, nr), lax.rem(c + dc + nc, nc)) for dr, dc in AROUND]
    peers = near[4:]
    peers += [(lax.rem(r + k, nr), c) for k in range(1, nr)]
    peers += [(r, lax.rem(c + k, nc)) for k in range(1, nc)]
    picked[...] = dot(rim_picks(rows, cols), patches[...]).astype(jnp.bfloat16).reshape(picked.shape)
    greet(peers)
    rim_copies = []
    for d, peer in enumerate(near):
        rim_copies.append(pltpu.make_async_remote_copy(
            src_ref=picked.at[d], dst_ref=rim_in.at[d], send_sem=rim_send.at[d],
            recv_sem=rim_recv.at[d], device_id=peer, device_id_type=MESH))
        rim_copies[-1].start()
    half = len(scratch) // 2
    row, col = scratch[:half], scratch[half:]
    parts = ((row, "col", nc, c, "row", nr, r, specs[0], 0), (col, "row", nr, r, "col", nc, c, specs[1], 2))
    for work, axis, n, me, chain, m, place, spec, first in parts:
        gather_weights(first, me, spec[3], spec[2], rank, state, dt_weight, dt_bias, decay, *work[13:17])
    front(dims, rim_copies, patches, rim_in, w_in, w_conv, extras, w_x, tissue,
          row[0], col[0], act, gate, frame)
    away = [swap(axis, n, work[0], work[1], *work[4:7]) for work, axis, n, *unused in parts]
    sums = []
    for p, (work, axis, n, me, chain, m, place, spec, first) in enumerate(parts):
        finish(away[p])
        first_pass(spec, m, place, work[1], *work[13:23], work[23])
        sums.append(spread(chain, m, work[23], work[10], work[11]))
    home = []
    for p, (work, axis, n, me, chain, m, place, spec, first) in enumerate(parts):
        finish(sums[p])
        second_pass(spec, m, place, *work[15:24], work[12], work[2])
        home.append(swap(axis, n, work[2], work[3], *work[7:10]))
    finish(home[0])
    flip = turn_back(rows, cols)
    each = inner // nc
    for g in range(nc):
        mixed[:, g * each:(g + 1) * each] = dot(flip, row[3][g])[:, :each]
    finish(home[1])
    each = inner // nr
    for g in range(nr):
        here = slice(g * each, (g + 1) * each)
        mixed[:, here] = mixed[:, here] + col[3][g].astype(jnp.float32)[:, :each]
    total = mixed[...] + extras[1:2, :] * act[...].astype(jnp.float32)
    centered = total - jnp.mean(total, axis=1, keepdims=True)
    variance = jnp.mean(centered * centered, axis=1, keepdims=True)
    normed = centered * lax.rsqrt(variance + 1e-05) * extras[2:3, :]
    gate_wide = gate[...].astype(jnp.float32)
    value = (normed * (gate_wide * jax.nn.sigmoid(gate_wide))).astype(jnp.bfloat16)
    result = dot(value, w_out[...]) * tissue_column(tissue, rows, cols)
    out[...] = result.astype(jnp.bfloat16)


def per_device(nr, nc, patches, tissue, in_weight, conv_weight, conv_bias, x_weight, dt_weight,
               dt_bias, decay_rate, skip_gain, norm_gain, out_weight):
    rows, cols, channels = patches.shape
    tokens = rows * cols
    inner = out_weight.shape[0]
    state = decay_rate.shape[2]
    rank = dt_weight.shape[1]
    bf, f32 = jnp.bfloat16, jnp.float32
    dma = pltpu.SemaphoreType.DMA
    dims = (rows, cols, inner, nr, nc, rank, state)
    specs, scratch = [], [
        pltpu.VMEM((8, cols, channels), bf), pltpu.VMEM((8, cols, channels), bf),
        pltpu.VMEM((rows + 2, -(-(cols + 2) // 8) * 8, inner), f32),
        pltpu.VMEM((tokens, inner), bf), pltpu.VMEM((tokens, inner), bf),
        pltpu.VMEM((tokens, inner), f32), dma((8,)), dma((8,))]
    for chains, n, m, length in ((rows, nc, nr, cols), (cols, nr, nc, rows)):
        each = inner // n
        width = lanes(each)
        steps = n * length
        specs.append((chains, steps, width, each, rank, state))
        count = chains * steps
        scratch += [
            pltpu.VMEM((n, tokens, 128 + width), bf), pltpu.VMEM((n, tokens, 128 + width), bf),
            pltpu.VMEM((n, tokens, width), bf), pltpu.VMEM((n, tokens, width), bf),
            dma((n,)), dma((n,)), dma((1,)), dma((n,)), dma((n,)), dma((1,)), dma((m,)), dma((m,)),
            pltpu.VMEM((state, chains, width), f32),
            pltpu.VMEM((128, 2 * width), bf), pltpu.VMEM((8, 2 * width), f32),
            pltpu.VMEM((state, 2 * width), f32), pltpu.VMEM((state, 8, 2 * width), f32),
            pltpu.VMEM((count, 2 * width), f32), pltpu.VMEM((count, 2 * width), f32),
            pltpu.VMEM((count, 128), f32), pltpu.VMEM((count, width), f32),
            pltpu.VMEM((2, state, chains, width), f32), pltpu.VMEM((2, chains, width), f32),
            pltpu.VMEM((m, 2, state + 8, width), f32)]
    extras = jnp.stack([conv_bias, skip_gain, norm_gain])
    out = pl.pallas_call(
        functools.partial(kernel, dims, specs),
        out_shape=jax.ShapeDtypeStruct((tokens, channels), bf),
        in_specs=[VMEM] * 10, out_specs=VMEM, scratch_shapes=scratch,
        compiler_params=pltpu.CompilerParams(
            collective_id=0, has_side_effects=True, vmem_limit_bytes=LIMIT),
        name="block",
    )(patches.reshape(tokens, channels), tissue, in_weight, conv_weight, extras, x_weight,
      dt_weight, dt_bias, jnp.transpose(decay_rate, (0, 2, 1)), out_weight)
    return out.reshape(rows, cols, channels)


def solution(mesh):
    grid = P("row", "col")
    return jax.shard_map(
        functools.partial(per_device, mesh.shape["row"], mesh.shape["col"]), mesh=mesh,
        in_specs=(P("row", "col", None), grid) + (P(),) * 10,
        out_specs=P("row", "col", None), check_vma=False)
```

```python
import functools
import math
import jax
import jax.numpy as jnp
from jax import lax
from jax.experimental import pallas as pl
from jax.experimental.pallas import tpu as pltpu
from jax.sharding import PartitionSpec as P

MESH = pl.DeviceIdType.MESH
VMEM = pl.BlockSpec(memory_space=pltpu.VMEM)
GROUP = 4
LIMIT = 56 * 1024 * 1024
LOG2E = math.log2(math.e)
AROUND = ((-1, 0), (1, 0), (0, -1), (0, 1), (-1, -1), (-1, 1), (1, -1), (1, 1))


def lanes(width):
    return -(-width // 128) * 128


def greet(peers):
    barrier = pltpu.get_barrier_semaphore()
    for peer in peers:
        pl.semaphore_signal(barrier, inc=1, device_id=peer, device_id_type=MESH)
    pl.semaphore_wait(barrier, len(peers))


def swap(axis, n, src, dst, send, recv, own):
    me = lax.axis_index(axis)
    copies = []
    for k in range(1, n):
        to = lax.rem(me + k, n)
        copies.append(pltpu.make_async_remote_copy(
            src_ref=src.at[to], dst_ref=dst.at[me], send_sem=send.at[k], recv_sem=recv.at[k],
            device_id={axis: to}, device_id_type=MESH))
    copies.append(pltpu.make_async_copy(src.at[me], dst.at[me], own.at[0]))
    for copy in copies:
        copy.start()
    return copies


def finish(copies):
    for copy in copies:
        copy.wait()


def spread(axis, n, slots, send, recv):
    me = lax.axis_index(axis)
    copies = []
    for k in range(1, n):
        copies.append(pltpu.make_async_remote_copy(
            src_ref=slots.at[me], dst_ref=slots.at[me], send_sem=send.at[k], recv_sem=recv.at[k],
            device_id={axis: lax.rem(me + k, n)}, device_id_type=MESH))
    for copy in copies:
        copy.start()
    return copies


def one_hot(hits):
    return hits.astype(jnp.float32).astype(jnp.bfloat16)


def iota(shape, dim):
    return lax.broadcasted_iota(jnp.int32, shape, dim)


def turn(rows, cols):
    count = rows * cols
    out = lax.broadcasted_iota(jnp.int32, (count, count), 0)
    src = lax.broadcasted_iota(jnp.int32, (count, count), 1)
    return (lax.rem(out, rows) * cols + lax.div(out, rows) == src).astype(jnp.float32).astype(jnp.bfloat16)


def turn_back(rows, cols):
    count = rows * cols
    out = lax.broadcasted_iota(jnp.int32, (count, count), 0)
    src = lax.broadcasted_iota(jnp.int32, (count, count), 1)
    return (lax.rem(out, cols) * rows + lax.div(out, cols) == src).astype(jnp.float32).astype(jnp.bfloat16)


def dot(a, b):
    return jnp.dot(a, b, preferred_element_type=jnp.float32)


def rim_picks(rows, cols):
    shape = (8 * cols, rows * cols)
    out, src = iota(shape, 0), iota(shape, 1)
    d, k = lax.div(out, cols), lax.rem(out, cols)
    last = (rows - 1) * cols
    token = jnp.where(d == 0, k, last + k)
    token = jnp.where(d == 2, k * cols, token)
    token = jnp.where(d == 3, k * cols + cols - 1, token)
    token = jnp.where(d == 4, 0, token)
    token = jnp.where(d == 5, cols - 1, token)
    token = jnp.where(d == 6, last, token)
    token = jnp.where(d == 7, rows * cols - 1, token)
    return one_hot(token == src)


def head_picks(columns, rank, state):
    shape = (columns, 256)
    src, out = iota(shape, 0), iota(shape, 1)
    wide = rank + 2 * state
    part, m = lax.div(out, 128), lax.rem(out, 128)
    base = 2 * part * wide
    at = jnp.where(m < 2 * state, base + rank + m, base + wide + rank + m - 2 * state)
    at = jnp.where(m >= 4 * state, base + m - 4 * state, at)
    at = jnp.where(m >= 4 * state + rank, base + wide + m - 4 * state - rank, at)
    at = jnp.where(m >= 4 * state + 2 * rank, -1, at)
    return one_hot(at == src)


def tissue_column(tissue, rows, cols):
    count = rows * cols
    up = one_hot(lax.div(iota((count, rows), 0), cols) == iota((count, rows), 1))
    spread_out = dot(up, tissue[...].astype(jnp.float32).astype(jnp.bfloat16))
    mine = lax.rem(iota((count, cols), 0), cols) == iota((count, cols), 1)
    return jnp.sum(jnp.where(mine, spread_out, 0.0), axis=1, keepdims=True)


def front(dims, rim_copies, patches, rim_in, w_in, w_conv, bias, w_x, tissue,
          msg_row, msg_col, act_out, gate_out, frame):
    rows, cols, inner, nr, nc, rank, state = dims
    tokens = rows * cols
    projected = dot(patches[...], w_in[...])
    gate_out[...] = projected[:, inner:].astype(jnp.bfloat16)
    body = projected[:, :inner].astype(jnp.bfloat16).astype(jnp.float32)
    frame[1:rows + 1, 1:cols + 1, :] = body.reshape(rows, cols, inner)
    finish(rim_copies)
    rim = dot(rim_in[...].reshape(8 * cols, -1), w_in[:, :inner])
    rim = rim.astype(jnp.bfloat16).astype(jnp.float32)
    r, c = lax.axis_index("row"), lax.axis_index("col")
    pieces = []
    for d, (dr, dc) in enumerate(AROUND):
        inside = (r - dr >= 0) & (r - dr < nr) & (c - dc >= 0) & (c - dc < nc)
        pieces.append(rim[d * cols:(d + 1) * cols] * jnp.where(inside, 1.0, 0.0))
    frame[rows + 1, 1:cols + 1, :] = pieces[0]
    frame[0, 1:cols + 1, :] = pieces[1]
    for i in range(rows):
        frame[i + 1, cols + 1:cols + 2, :] = pieces[2][i:i + 1]
        frame[i + 1, 0:1, :] = pieces[3][i:i + 1]
    frame[rows + 1, cols + 1:cols + 2, :] = pieces[4][0:1]
    frame[rows + 1, 0:1, :] = pieces[5][0:1]
    frame[0, cols + 1:cols + 2, :] = pieces[6][0:1]
    frame[0, 0:1, :] = pieces[7][0:1]
    total = jnp.zeros((rows, cols, inner), jnp.float32) + bias[...].reshape(1, inner)
    for i in range(3):
        for j in range(3):
            total = total + frame[i:i + rows, j:j + cols, :] * w_conv[i, j:j + 1, :]
    act = (total * jax.nn.sigmoid(total)).astype(jnp.bfloat16).reshape(tokens, inner)
    act_out[...] = act
    head = lax.dot_general(act, w_x[...], (((1,), (1,)), ((), ())),
                           preferred_element_type=jnp.float32).astype(jnp.bfloat16)
    head = dot(head, head_picks(w_x.shape[0], rank, state))
    mark = tissue_column(tissue, rows, cols)
    place = lax.rem(iota((tokens, 256), 1), 128)
    head = jnp.where(place == 4 * state + 2 * rank, mark, head).astype(jnp.bfloat16)
    flip = turn(rows, cols)
    head_row = dot(flip, head[:, :128]).astype(jnp.bfloat16)
    act_row = dot(flip, act).astype(jnp.bfloat16)
    for msg, n, top, values in ((msg_row, nc, head_row, act_row), (msg_col, nr, head[:, 128:], act)):
        each = inner // n
        for g in range(n):
            msg[g, :, 0:128] = top
            msg[g, :, 128:128 + each] = values[:, g * each:(g + 1) * each]


def pick_exact(values, picks):
    high = values.astype(jnp.bfloat16)
    rest = values - high.astype(jnp.float32)
    middle = rest.astype(jnp.bfloat16)
    low = (rest - middle.astype(jnp.float32)).astype(jnp.bfloat16)
    return dot(high, picks) + dot(middle, picks) + dot(low, picks)


def gather_weights(first, place, each, width, rank, state, dt_weight, dt_bias, decay,
                   wd_s, bias_s, nd_s, ndb_s):
    inner = dt_weight.shape[2]
    shape = (inner, width)
    picks = one_hot((iota(shape, 0) == iota(shape, 1) + place * each) & (iota(shape, 1) < each))
    top = 4 * state
    for b in range(2):
        here = slice(b * width, (b + 1) * width)
        w = dot(dt_weight[first + b], picks)
        above = top + b * rank
        w = jnp.concatenate([jnp.zeros((above, width), jnp.float32), w,
                             jnp.zeros((128 - above - rank, width), jnp.float32)], axis=0)
        wd_s[:, here] = w.astype(jnp.bfloat16)
        bias = jnp.broadcast_to(dt_bias[first + b:first + b + 1, :], (8, inner))
        bias_s[:, here] = pick_exact(bias, picks)
        rate = pick_exact(decay[first + b], picks) * -LOG2E
        nd_s[:, here] = rate
        for s in range(state):
            ndb_s[s, :, here] = jnp.broadcast_to(rate[s:s + 1], (8, width))


def full(rate, chains):
    return rate if chains == 8 else jnp.concatenate([rate] * (chains // 8), axis=0)


def chain_pass(spec, refs, backward, states, outputs):
    chains, steps, width, state = spec
    dt_ref, du_ref, bc_ref, ndb_ref, y_ref = refs
    b_at = 2 * state if backward else 0
    c_at = b_at + state
    col = width if backward else 0
    ends = []
    summed = None
    for low in range(0, state, GROUP):
        group = range(low, low + GROUP)
        rates = [full(ndb_ref[s, :, col:col + width], chains) for s in group]
        write = low == 0 and not backward
        count = low == 0 and not outputs

        def one(i, carry, group=group, rates=rates, write=write, count=count):
            held, total = carry
            t = steps - 1 - i if backward else i
            here = pl.ds(pl.multiple_of(t * chains, chains), chains)
            dt = dt_ref[here, col:col + width]
            du = du_ref[here, col:col + width]
            bc = bc_ref[here, :]
            fresh, terms = [], []
            for s, rate, before in zip(group, rates, held):
                h = jnp.exp2(rate * dt) * before + du * bc[:, b_at + s:b_at + s + 1]
                fresh.append(h)
                if outputs:
                    terms.append(h * bc[:, c_at + s:c_at + s + 1])
            if outputs:
                y = (terms[0] + terms[1]) + (terms[2] + terms[3])
                y_ref[here, :] = y if write else y_ref[here, :] + y
            return tuple(fresh), total + dt if count else total

        start = jnp.zeros((chains, width), jnp.float32) if count else 0
        held, total = lax.fori_loop(0, steps, one, (tuple(states[low:low + GROUP]), start), unroll=8)
        ends += held
        summed = total if count else summed
    return ends, summed


def shifted(values, by, backward):
    edge = jnp.zeros((by, values.shape[1]), jnp.float32)
    if backward:
        return jnp.concatenate([values[by:], edge], axis=0)
    return jnp.concatenate([edge, values[:-by]], axis=0)


def first_pass(spec, n, me, got, wd_s, bias_s, nd_s, ndb_s, dt_s, du_s, bc_s, y_s, entry_s, sum_s, slots):
    chains, steps, width, each, rank, state = spec
    senders, block = got.shape[0], got.shape[1]
    mark_at = 4 * state + 2 * rank
    for g in range(senders):
        here = slice(g * block, (g + 1) * block)
        head = got[g, :, 0:128]
        wide = head.astype(jnp.float32)
        bc_s[here, :] = wide
        x = dot(head, wd_s[...]) + bias_s[0:1, :]
        dt = (jnp.maximum(x, 0.0) + jnp.log1p(jnp.exp(-jnp.abs(x)))) * wide[:, mark_at:mark_at + 1]
        dt_s[here, :] = dt
        act = got[g, :, 128:128 + width].astype(jnp.float32)
        if each < width:
            act = jnp.where(iota((block, width), 1) < each, act, 0.0)
        du_s[here, 0:width] = dt[:, 0:width] * act
        du_s[here, width:2 * width] = dt[:, width:2 * width] * act
    for b in range(2):
        col = b * width
        zero = [jnp.zeros((chains, width), jnp.float32)] * state
        ends, total = chain_pass((chains, steps, width, state),
                                 (dt_s, du_s, bc_s, ndb_s, y_s), b == 1, zero, False)
        rates = [full(ndb_s[s, :, col:col + width], chains) for s in range(state)]
        by = 1
        while by < chains:
            ends = [jnp.exp2(rate * total) * shifted(end, by, b == 1) + end
                    for rate, end in zip(rates, ends)]
            total = total + shifted(total, by, b == 1)
            by *= 2
        last = 0 if b else chains - 1
        for s in range(state):
            slots[me, b, s:s + 1, :] = ends[s][last:last + 1]
            entry_s[b, s] = shifted(ends[s], 1, b == 1)
        slots[me, b, state:state + 8, :] = jnp.broadcast_to(total[last:last + 1], (8, width))
        sum_s[b] = shifted(total, 1, b == 1)


def second_pass(spec, n, me, nd_s, ndb_s, dt_s, du_s, bc_s, y_s, entry_s, sum_s, slots, y_out):
    chains, steps, width, each, rank, state = spec
    for b in range(2):
        col = b * width
        nd = nd_s[:, col:col + width]
        held = jnp.zeros((state, width), jnp.float32)
        for q in (range(n - 1, -1, -1) if b else range(n)):
            ahead = (q > me) if b else (q < me)
            keep = jnp.where(ahead, 1.0, 0.0)
            after = jnp.exp2(nd * slots[q, b, state:state + 1, :]) * held + slots[q, b, 0:state, :]
            held = held + keep * (after - held)
        start = [
            jnp.exp2(full(ndb_s[s, :, col:col + width], chains) * sum_s[b]) * held[s:s + 1]
            + entry_s[b, s] for s in range(state)]
        chain_pass((chains, steps, width, state),
                   (dt_s, du_s, bc_s, ndb_s, y_s), b == 1, start, True)
    groups, count = y_out.shape[0], y_out.shape[1]
    for g in range(groups):
        y_out[g] = y_s[g * count:(g + 1) * count, :].astype(jnp.bfloat16)


def kernel(dims, specs, patches, tissue, w_in, w_conv, bias, skip, gain, w_x, dt_weight, dt_bias, decay,
           w_out, out, picked, rim_in, frame, act, gate, mixed, rim_send, rim_recv, *scratch):
    rows, cols, inner, nr, nc, rank, state = dims
    r, c = lax.axis_index("row"), lax.axis_index("col")
    near = [(lax.rem(r + dr + nr, nr), lax.rem(c + dc + nc, nc)) for dr, dc in AROUND]
    peers = near[4:]
    peers += [(lax.rem(r + k, nr), c) for k in range(1, nr)]
    peers += [(r, lax.rem(c + k, nc)) for k in range(1, nc)]
    picked[...] = dot(rim_picks(rows, cols), patches[...]).astype(jnp.bfloat16).reshape(picked.shape)
    greet(peers)
    rim_copies = []
    for d, peer in enumerate(near):
        rim_copies.append(pltpu.make_async_remote_copy(
            src_ref=picked.at[d], dst_ref=rim_in.at[d], send_sem=rim_send.at[d],
            recv_sem=rim_recv.at[d], device_id=peer, device_id_type=MESH))
        rim_copies[-1].start()
    half = len(scratch) // 2
    row, col = scratch[:half], scratch[half:]
    parts = ((row, "col", nc, c, "row", nr, r, specs[0], 0), (col, "row", nr, r, "col", nc, c, specs[1], 2))
    front(dims, rim_copies, patches, rim_in, w_in, w_conv, bias, w_x, tissue,
          row[0], col[0], act, gate, frame)
    away = [swap(axis, n, work[0], work[1], *work[4:7]) for work, axis, n, *unused in parts]
    for work, axis, n, me, chain, m, place, spec, first in parts:
        gather_weights(first, me, spec[3], spec[2], rank, state, dt_weight, dt_bias, decay, *work[13:17])
    sums = []
    for p, (work, axis, n, me, chain, m, place, spec, first) in enumerate(parts):
        finish(away[p])
        first_pass(spec, m, place, work[1], *work[13:23], work[23])
        sums.append(spread(chain, m, work[23], work[10], work[11]))
    home = []
    for p, (work, axis, n, me, chain, m, place, spec, first) in enumerate(parts):
        finish(sums[p])
        second_pass(spec, m, place, *work[15:24], work[2])
        home.append(swap(axis, n, work[2], work[3], *work[7:10]))
    finish(home[0])
    flip = turn_back(rows, cols)
    each = inner // nc
    for g in range(nc):
        mixed[:, g * each:(g + 1) * each] = dot(flip, row[3][g])[:, :each]
    finish(home[1])
    each = inner // nr
    for g in range(nr):
        here = slice(g * each, (g + 1) * each)
        mixed[:, here] = mixed[:, here] + col[3][g].astype(jnp.float32)[:, :each]
    total = mixed[...] + skip[...].reshape(1, inner) * act[...].astype(jnp.float32)
    centered = total - jnp.mean(total, axis=1, keepdims=True)
    variance = jnp.mean(centered * centered, axis=1, keepdims=True)
    normed = centered * lax.rsqrt(variance + 1e-05) * gain[...].reshape(1, inner)
    gate_wide = gate[...].astype(jnp.float32)
    value = (normed * (gate_wide * jax.nn.sigmoid(gate_wide))).astype(jnp.bfloat16)
    result = dot(value, w_out[...]) * tissue_column(tissue, rows, cols)
    out[...] = result


def per_device(nr, nc, patches, tissue, in_weight, conv_weight, conv_bias, x_weight, dt_weight,
               dt_bias, decay_rate, skip_gain, norm_gain, out_weight):
    rows, cols, channels = patches.shape
    tokens = rows * cols
    inner = out_weight.shape[0]
    state = decay_rate.shape[2]
    rank = dt_weight.shape[1]
    bf, f32 = jnp.bfloat16, jnp.float32
    dma = pltpu.SemaphoreType.DMA
    dims = (rows, cols, inner, nr, nc, rank, state)
    specs, scratch = [], [
        pltpu.VMEM((8, cols, channels), bf), pltpu.VMEM((8, cols, channels), bf),
        pltpu.VMEM((rows + 2, -(-(cols + 2) // 8) * 8, inner), f32),
        pltpu.VMEM((tokens, inner), bf), pltpu.VMEM((tokens, inner), bf),
        pltpu.VMEM((tokens, inner), f32), dma((8,)), dma((8,))]
    for chains, n, m, length in ((rows, nc, nr, cols), (cols, nr, nc, rows)):
        each = inner // n
        width = lanes(each)
        steps = n * length
        specs.append((chains, steps, width, each, rank, state))
        count = chains * steps
        scratch += [
            pltpu.VMEM((n, tokens, 128 + width), bf), pltpu.VMEM((n, tokens, 128 + width), bf),
            pltpu.VMEM((n, tokens, width), bf), pltpu.VMEM((n, tokens, width), bf),
            dma((n,)), dma((n,)), dma((1,)), dma((n,)), dma((n,)), dma((1,)), dma((m,)), dma((m,)),
            dma((1,)),
            pltpu.VMEM((128, 2 * width), bf), pltpu.VMEM((8, 2 * width), f32),
            pltpu.VMEM((state, 2 * width), f32), pltpu.VMEM((state, 8, 2 * width), f32),
            pltpu.VMEM((count, 2 * width), f32), pltpu.VMEM((count, 2 * width), f32),
            pltpu.VMEM((count, 128), f32), pltpu.VMEM((count, width), f32),
            pltpu.VMEM((2, state, chains, width), f32), pltpu.VMEM((2, chains, width), f32),
            pltpu.VMEM((m, 2, state + 8, width), f32)]
    out = pl.pallas_call(
        functools.partial(kernel, dims, specs),
        out_shape=jax.ShapeDtypeStruct((tokens, channels), f32),
        in_specs=[VMEM] * 12, out_specs=VMEM, scratch_shapes=scratch,
        compiler_params=pltpu.CompilerParams(
            collective_id=0, has_side_effects=True, vmem_limit_bytes=LIMIT),
        name="block",
    )(patches.reshape(tokens, channels), tissue, in_weight, conv_weight, conv_bias, skip_gain, norm_gain, x_weight.T,
      dt_weight, dt_bias, jnp.transpose(decay_rate, (0, 2, 1)), out_weight)
    return out.astype(bf).reshape(rows, cols, channels)


def solution(mesh):
    grid = P("row", "col")
    return jax.shard_map(
        functools.partial(per_device, mesh.shape["row"], mesh.shape["col"]), mesh=mesh,
        in_specs=(P("row", "col", None), grid) + (P(),) * 10,
        out_specs=P("row", "col", None), check_vma=False)
```

```python
import functools
import math
import jax
import jax.numpy as jnp
from jax import lax
from jax.experimental import pallas as pl
from jax.experimental.pallas import tpu as pltpu
from jax.sharding import PartitionSpec as P

MESH = pl.DeviceIdType.MESH
VMEM = pl.BlockSpec(memory_space=pltpu.VMEM)
LIMIT = 56 * 1024 * 1024
LOG2E = math.log2(math.e)
AROUND = ((-1, 0), (1, 0), (0, -1), (0, 1), (-1, -1), (-1, 1), (1, -1), (1, 1))


def lanes(width):
    return -(-width // 128) * 128


def greet(peers):
    barrier = pltpu.get_barrier_semaphore()
    for peer in peers:
        pl.semaphore_signal(barrier, inc=1, device_id=peer, device_id_type=MESH)
    pl.semaphore_wait(barrier, len(peers))


def swap(axis, n, src, dst, send, recv, own):
    me = lax.axis_index(axis)
    copies = []
    for k in range(1, n):
        to = lax.rem(me + k, n)
        copies.append(pltpu.make_async_remote_copy(
            src_ref=src.at[to], dst_ref=dst.at[me], send_sem=send.at[k], recv_sem=recv.at[k],
            device_id={axis: to}, device_id_type=MESH))
    copies.append(pltpu.make_async_copy(src.at[me], dst.at[me], own.at[0]))
    for copy in copies:
        copy.start()
    return copies


def finish(copies):
    for copy in copies:
        copy.wait()


def spread(axis, n, slots, send, recv):
    me = lax.axis_index(axis)
    copies = []
    for k in range(1, n):
        copies.append(pltpu.make_async_remote_copy(
            src_ref=slots.at[me], dst_ref=slots.at[me], send_sem=send.at[k], recv_sem=recv.at[k],
            device_id={axis: lax.rem(me + k, n)}, device_id_type=MESH))
    for copy in copies:
        copy.start()
    return copies


def one_hot(hits):
    return hits.astype(jnp.float32).astype(jnp.bfloat16)


def iota(shape, dim):
    return lax.broadcasted_iota(jnp.int32, shape, dim)


def turn(rows, cols):
    count = rows * cols
    out = lax.broadcasted_iota(jnp.int32, (count, count), 0)
    src = lax.broadcasted_iota(jnp.int32, (count, count), 1)
    return (lax.rem(out, rows) * cols + lax.div(out, rows) == src).astype(jnp.float32).astype(jnp.bfloat16)


def turn_back(rows, cols):
    count = rows * cols
    out = lax.broadcasted_iota(jnp.int32, (count, count), 0)
    src = lax.broadcasted_iota(jnp.int32, (count, count), 1)
    return (lax.rem(out, cols) * rows + lax.div(out, cols) == src).astype(jnp.float32).astype(jnp.bfloat16)


def dot(a, b):
    return jnp.dot(a, b, preferred_element_type=jnp.float32)


def rim_picks(rows, cols):
    shape = (8 * cols, rows * cols)
    out, src = iota(shape, 0), iota(shape, 1)
    d, k = lax.div(out, cols), lax.rem(out, cols)
    last = (rows - 1) * cols
    token = jnp.where(d == 0, k, last + k)
    token = jnp.where(d == 2, k * cols, token)
    token = jnp.where(d == 3, k * cols + cols - 1, token)
    token = jnp.where(d == 4, 0, token)
    token = jnp.where(d == 5, cols - 1, token)
    token = jnp.where(d == 6, last, token)
    token = jnp.where(d == 7, rows * cols - 1, token)
    return one_hot(token == src)


def head_picks(columns, rank, state):
    shape = (columns, 256)
    src, out = iota(shape, 0), iota(shape, 1)
    wide = rank + 2 * state
    part, m = lax.div(out, 128), lax.rem(out, 128)
    base = 2 * part * wide
    at = jnp.where(m < 2 * state, base + rank + m, base + wide + rank + m - 2 * state)
    at = jnp.where(m >= 4 * state, base + m - 4 * state, at)
    at = jnp.where(m >= 4 * state + rank, base + wide + m - 4 * state - rank, at)
    at = jnp.where(m >= 4 * state + 2 * rank, -1, at)
    return one_hot(at == src)


def tissue_column(tissue, rows, cols):
    count = rows * cols
    up = one_hot(lax.div(iota((count, rows), 0), cols) == iota((count, rows), 1))
    spread_out = dot(up, tissue[...].astype(jnp.float32).astype(jnp.bfloat16))
    mine = lax.rem(iota((count, cols), 0), cols) == iota((count, cols), 1)
    return jnp.sum(jnp.where(mine, spread_out, 0.0), axis=1, keepdims=True)


def front(dims, rim_copies, patches, rim_in, w_in, w_conv, bias, w_x, tissue,
          msg_row, msg_col, act_out, gate_out, frame):
    rows, cols, inner, nr, nc, rank, state = dims
    tokens = rows * cols
    projected = dot(patches[...], w_in[...])
    gate_out[...] = projected[:, inner:].astype(jnp.bfloat16)
    body = projected[:, :inner].astype(jnp.bfloat16).astype(jnp.float32)
    frame[1:rows + 1, 1:cols + 1, :] = body.reshape(rows, cols, inner)
    finish(rim_copies)
    rim = dot(rim_in[...].reshape(8 * cols, -1), w_in[:, :inner])
    rim = rim.astype(jnp.bfloat16).astype(jnp.float32)
    r, c = lax.axis_index("row"), lax.axis_index("col")
    pieces = []
    for d, (dr, dc) in enumerate(AROUND):
        inside = (r - dr >= 0) & (r - dr < nr) & (c - dc >= 0) & (c - dc < nc)
        pieces.append(rim[d * cols:(d + 1) * cols] * jnp.where(inside, 1.0, 0.0))
    frame[rows + 1, 1:cols + 1, :] = pieces[0]
    frame[0, 1:cols + 1, :] = pieces[1]
    for i in range(rows):
        frame[i + 1, cols + 1:cols + 2, :] = pieces[2][i:i + 1]
        frame[i + 1, 0:1, :] = pieces[3][i:i + 1]
    frame[rows + 1, cols + 1:cols + 2, :] = pieces[4][0:1]
    frame[rows + 1, 0:1, :] = pieces[5][0:1]
    frame[0, cols + 1:cols + 2, :] = pieces[6][0:1]
    frame[0, 0:1, :] = pieces[7][0:1]
    total = jnp.zeros((rows, cols, inner), jnp.float32) + bias[...].reshape(1, inner)
    for i in range(3):
        for j in range(3):
            total = total + frame[i:i + rows, j:j + cols, :] * w_conv[i, j:j + 1, :]
    act = (total * jax.nn.sigmoid(total)).astype(jnp.bfloat16).reshape(tokens, inner)
    act_out[...] = act
    head = lax.dot_general(act, w_x[...], (((1,), (1,)), ((), ())),
                           preferred_element_type=jnp.float32).astype(jnp.bfloat16)
    head = dot(head, head_picks(w_x.shape[0], rank, state))
    mark = tissue_column(tissue, rows, cols)
    place = lax.rem(iota((tokens, 256), 1), 128)
    head = jnp.where(place == 4 * state + 2 * rank, mark, head).astype(jnp.bfloat16)
    flip = turn(rows, cols)
    head_row = dot(flip, head[:, :128]).astype(jnp.bfloat16)
    act_row = dot(flip, act).astype(jnp.bfloat16)
    for msg, n, top, values in ((msg_row, nc, head_row, act_row), (msg_col, nr, head[:, 128:], act)):
        each = inner // n
        for g in range(n):
            msg[g, :, 0:128] = top
            msg[g, :, 128:128 + each] = values[:, g * each:(g + 1) * each]


def pick_exact(values, picks):
    high = values.astype(jnp.bfloat16)
    rest = values - high.astype(jnp.float32)
    middle = rest.astype(jnp.bfloat16)
    low = (rest - middle.astype(jnp.float32)).astype(jnp.bfloat16)
    return dot(high, picks) + dot(middle, picks) + dot(low, picks)


def gather_weights(first, place, each, width, rank, state, dt_weight, dt_bias, decay,
                   wd_s, bias_s, nd_s, ndb_s):
    inner = dt_weight.shape[2]
    shape = (inner, width)
    picks = one_hot((iota(shape, 0) == iota(shape, 1) + place * each) & (iota(shape, 1) < each))
    top = 4 * state
    for b in range(2):
        here = slice(b * width, (b + 1) * width)
        w = dot(dt_weight[first + b], picks)
        above = top + b * rank
        w = jnp.concatenate([jnp.zeros((above, width), jnp.float32), w,
                             jnp.zeros((128 - above - rank, width), jnp.float32)], axis=0)
        wd_s[:, here] = w.astype(jnp.bfloat16)
        bias = jnp.broadcast_to(dt_bias[first + b:first + b + 1, :], (8, inner))
        bias_s[:, here] = pick_exact(bias, picks)
        rate = pick_exact(decay[first + b], picks) * -LOG2E
        nd_s[:, here] = rate
        for s in range(state):
            ndb_s[s, :, here] = jnp.broadcast_to(rate[s:s + 1], (8, width))


def full(rate, chains):
    return rate if chains == 8 else jnp.concatenate([rate] * (chains // 8), axis=0)


def chain_pass(spec, refs, backward, states, outputs):
    chains, steps, width, state = spec
    dt_ref, du_ref, bc_ref, ndb_ref, y_ref = refs
    b_at = 2 * state if backward else 0
    c_at = b_at + state
    col = width if backward else 0

    def one(i, carry):
        held, total = carry
        t = steps - 1 - i if backward else i
        here = pl.ds(pl.multiple_of(t * chains, chains), chains)
        dt = dt_ref[here, col:col + width]
        du = du_ref[here, col:col + width]
        bc = bc_ref[here, :]
        y = y_ref[here, :] if outputs and backward else None
        fresh = []
        for s in range(state):
            rate = full(ndb_ref[s, :, col:col + width], chains)
            h = jnp.exp2(rate * dt) * held[s] + du * bc[:, b_at + s:b_at + s + 1]
            fresh.append(h)
            if outputs:
                term = h * bc[:, c_at + s:c_at + s + 1]
                y = term if y is None else y + term
        if outputs:
            y_ref[here, :] = y
        return tuple(fresh), total if outputs else total + dt

    start = 0 if outputs else jnp.zeros((chains, width), jnp.float32)
    return lax.fori_loop(0, steps, one, (tuple(states), start), unroll=8)


def shifted(values, by, backward):
    edge = jnp.zeros((by, values.shape[1]), jnp.float32)
    if backward:
        return jnp.concatenate([values[by:], edge], axis=0)
    return jnp.concatenate([edge, values[:-by]], axis=0)


def first_pass(spec, n, me, got, wd_s, bias_s, nd_s, ndb_s, dt_s, du_s, bc_s, y_s, entry_s, sum_s, slots):
    chains, steps, width, each, rank, state = spec
    senders, block = got.shape[0], got.shape[1]
    mark_at = 4 * state + 2 * rank
    for g in range(senders):
        here = slice(g * block, (g + 1) * block)
        head = got[g, :, 0:128]
        wide = head.astype(jnp.float32)
        bc_s[here, :] = wide
        x = dot(head, wd_s[...]) + bias_s[0:1, :]
        dt = (jnp.maximum(x, 0.0) + jnp.log1p(jnp.exp(-jnp.abs(x)))) * wide[:, mark_at:mark_at + 1]
        dt_s[here, :] = dt
        act = got[g, :, 128:128 + width].astype(jnp.float32)
        if each < width:
            act = jnp.where(iota((block, width), 1) < each, act, 0.0)
        du_s[here, 0:width] = dt[:, 0:width] * act
        du_s[here, width:2 * width] = dt[:, width:2 * width] * act
    for b in range(2):
        col = b * width
        zero = [jnp.zeros((chains, width), jnp.float32)] * state
        ends, total = chain_pass((chains, steps, width, state),
                                 (dt_s, du_s, bc_s, ndb_s, y_s), b == 1, zero, False)
        rates = [full(ndb_s[s, :, col:col + width], chains) for s in range(state)]
        by = 1
        while by < chains:
            ends = [jnp.exp2(rate * total) * shifted(end, by, b == 1) + end
                    for rate, end in zip(rates, ends)]
            total = total + shifted(total, by, b == 1)
            by *= 2
        last = 0 if b else chains - 1
        for s in range(state):
            slots[me, b, s:s + 1, :] = ends[s][last:last + 1]
            entry_s[b, s] = shifted(ends[s], 1, b == 1)
        slots[me, b, state:state + 8, :] = jnp.broadcast_to(total[last:last + 1], (8, width))
        sum_s[b] = shifted(total, 1, b == 1)


def second_pass(spec, n, me, nd_s, ndb_s, dt_s, du_s, bc_s, y_s, entry_s, sum_s, slots, y_out):
    chains, steps, width, each, rank, state = spec
    for b in range(2):
        col = b * width
        nd = nd_s[:, col:col + width]
        held = jnp.zeros((state, width), jnp.float32)
        for q in (range(n - 1, -1, -1) if b else range(n)):
            ahead = (q > me) if b else (q < me)
            keep = jnp.where(ahead, 1.0, 0.0)
            after = jnp.exp2(nd * slots[q, b, state:state + 1, :]) * held + slots[q, b, 0:state, :]
            held = held + keep * (after - held)
        start = [
            jnp.exp2(full(ndb_s[s, :, col:col + width], chains) * sum_s[b]) * held[s:s + 1]
            + entry_s[b, s] for s in range(state)]
        chain_pass((chains, steps, width, state),
                   (dt_s, du_s, bc_s, ndb_s, y_s), b == 1, start, True)
    groups, count = y_out.shape[0], y_out.shape[1]
    for g in range(groups):
        y_out[g] = y_s[g * count:(g + 1) * count, :].astype(jnp.bfloat16)


def kernel(dims, specs, patches, tissue, w_in, w_conv, bias, skip, gain, w_x, dt_weight, dt_bias, decay,
           w_out, out, picked, rim_in, frame, act, gate, mixed, rim_send, rim_recv, *scratch):
    rows, cols, inner, nr, nc, rank, state = dims
    r, c = lax.axis_index("row"), lax.axis_index("col")
    near = [(lax.rem(r + dr + nr, nr), lax.rem(c + dc + nc, nc)) for dr, dc in AROUND]
    peers = near[4:]
    peers += [(lax.rem(r + k, nr), c) for k in range(1, nr)]
    peers += [(r, lax.rem(c + k, nc)) for k in range(1, nc)]
    picked[...] = dot(rim_picks(rows, cols), patches[...]).astype(jnp.bfloat16).reshape(picked.shape)
    greet(peers)
    rim_copies = []
    for d, peer in enumerate(near):
        rim_copies.append(pltpu.make_async_remote_copy(
            src_ref=picked.at[d], dst_ref=rim_in.at[d], send_sem=rim_send.at[d],
            recv_sem=rim_recv.at[d], device_id=peer, device_id_type=MESH))
        rim_copies[-1].start()
    half = len(scratch) // 2
    row, col = scratch[:half], scratch[half:]
    parts = ((row, "col", nc, c, "row", nr, r, specs[0], 0), (col, "row", nr, r, "col", nc, c, specs[1], 2))
    front(dims, rim_copies, patches, rim_in, w_in, w_conv, bias, w_x, tissue,
          row[0], col[0], act, gate, frame)
    away = [swap(axis, n, work[0], work[1], *work[4:7]) for work, axis, n, *unused in parts]
    for work, axis, n, me, chain, m, place, spec, first in parts:
        gather_weights(first, me, spec[3], spec[2], rank, state, dt_weight, dt_bias, decay, *work[13:17])
    sums = []
    for p, (work, axis, n, me, chain, m, place, spec, first) in enumerate(parts):
        finish(away[p])
        first_pass(spec, m, place, work[1], *work[13:23], work[23])
        sums.append(spread(chain, m, work[23], work[10], work[11]))
    home = []
    for p, (work, axis, n, me, chain, m, place, spec, first) in enumerate(parts):
        finish(sums[p])
        second_pass(spec, m, place, *work[15:24], work[2])
        home.append(swap(axis, n, work[2], work[3], *work[7:10]))
    finish(home[0])
    flip = turn_back(rows, cols)
    each = inner // nc
    for g in range(nc):
        mixed[:, g * each:(g + 1) * each] = dot(flip, row[3][g])[:, :each]
    finish(home[1])
    each = inner // nr
    for g in range(nr):
        here = slice(g * each, (g + 1) * each)
        mixed[:, here] = mixed[:, here] + col[3][g].astype(jnp.float32)[:, :each]
    total = mixed[...] + skip[...].reshape(1, inner) * act[...].astype(jnp.float32)
    centered = total - jnp.mean(total, axis=1, keepdims=True)
    variance = jnp.mean(centered * centered, axis=1, keepdims=True)
    normed = centered * lax.rsqrt(variance + 1e-05) * gain[...].reshape(1, inner)
    gate_wide = gate[...].astype(jnp.float32)
    value = (normed * (gate_wide * jax.nn.sigmoid(gate_wide))).astype(jnp.bfloat16)
    result = dot(value, w_out[...]) * tissue_column(tissue, rows, cols)
    out[...] = result


def per_device(nr, nc, patches, tissue, in_weight, conv_weight, conv_bias, x_weight, dt_weight,
               dt_bias, decay_rate, skip_gain, norm_gain, out_weight):
    rows, cols, channels = patches.shape
    tokens = rows * cols
    inner = out_weight.shape[0]
    state = decay_rate.shape[2]
    rank = dt_weight.shape[1]
    bf, f32 = jnp.bfloat16, jnp.float32
    dma = pltpu.SemaphoreType.DMA
    dims = (rows, cols, inner, nr, nc, rank, state)
    specs, scratch = [], [
        pltpu.VMEM((8, cols, channels), bf), pltpu.VMEM((8, cols, channels), bf),
        pltpu.VMEM((rows + 2, -(-(cols + 2) // 8) * 8, inner), f32),
        pltpu.VMEM((tokens, inner), bf), pltpu.VMEM((tokens, inner), bf),
        pltpu.VMEM((tokens, inner), f32), dma((8,)), dma((8,))]
    for chains, n, m, length in ((rows, nc, nr, cols), (cols, nr, nc, rows)):
        each = inner // n
        width = lanes(each)
        steps = n * length
        specs.append((chains, steps, width, each, rank, state))
        count = chains * steps
        scratch += [
            pltpu.VMEM((n, tokens, 128 + width), bf), pltpu.VMEM((n, tokens, 128 + width), bf),
            pltpu.VMEM((n, tokens, width), bf), pltpu.VMEM((n, tokens, width), bf),
            dma((n,)), dma((n,)), dma((1,)), dma((n,)), dma((n,)), dma((1,)), dma((m,)), dma((m,)),
            dma((1,)),
            pltpu.VMEM((128, 2 * width), bf), pltpu.VMEM((8, 2 * width), f32),
            pltpu.VMEM((state, 2 * width), f32), pltpu.VMEM((state, 8, 2 * width), f32),
            pltpu.VMEM((count, 2 * width), f32), pltpu.VMEM((count, 2 * width), f32),
            pltpu.VMEM((count, 128), f32), pltpu.VMEM((count, width), f32),
            pltpu.VMEM((2, state, chains, width), f32), pltpu.VMEM((2, chains, width), f32),
            pltpu.VMEM((m, 2, state + 8, width), f32)]
    out = pl.pallas_call(
        functools.partial(kernel, dims, specs),
        out_shape=jax.ShapeDtypeStruct((tokens, channels), f32),
        in_specs=[VMEM] * 12, out_specs=VMEM, scratch_shapes=scratch,
        compiler_params=pltpu.CompilerParams(
            collective_id=0, has_side_effects=True, vmem_limit_bytes=LIMIT),
        name="block",
    )(patches.reshape(tokens, channels), tissue, in_weight, conv_weight, conv_bias, skip_gain, norm_gain, x_weight.T,
      dt_weight, dt_bias, jnp.transpose(decay_rate, (0, 2, 1)), out_weight)
    return out.astype(bf).reshape(rows, cols, channels)


def solution(mesh):
    grid = P("row", "col")
    return jax.shard_map(
        functools.partial(per_device, mesh.shape["row"], mesh.shape["col"]), mesh=mesh,
        in_specs=(P("row", "col", None), grid) + (P(),) * 10,
        out_specs=P("row", "col", None), check_vma=False)
```

```python
import functools
import math
import jax
import jax.numpy as jnp
from jax import lax
from jax.experimental import pallas as pl
from jax.experimental.pallas import tpu as pltpu
from jax.sharding import PartitionSpec as P

MESH = pl.DeviceIdType.MESH
VMEM = pl.BlockSpec(memory_space=pltpu.VMEM)
LIMIT = 56 * 1024 * 1024
LOG2E = math.log2(math.e)
AROUND = ((-1, 0), (1, 0), (0, -1), (0, 1), (-1, -1), (-1, 1), (1, -1), (1, 1))


def lanes(width):
    return -(-width // 128) * 128


def greet(peers):
    barrier = pltpu.get_barrier_semaphore()
    for peer in peers:
        pl.semaphore_signal(barrier, inc=1, device_id=peer, device_id_type=MESH)
    pl.semaphore_wait(barrier, len(peers))


def swap(axis, n, src, dst, send, recv, own):
    me = lax.axis_index(axis)
    copies = []
    for k in range(1, n):
        to = lax.rem(me + k, n)
        copies.append(pltpu.make_async_remote_copy(
            src_ref=src.at[to], dst_ref=dst.at[me], send_sem=send.at[k], recv_sem=recv.at[k],
            device_id={axis: to}, device_id_type=MESH))
    copies.append(pltpu.make_async_copy(src.at[me], dst.at[me], own.at[0]))
    for copy in copies:
        copy.start()
    return copies


def finish(copies):
    for copy in copies:
        copy.wait()


def spread(axis, n, slots, send, recv):
    me = lax.axis_index(axis)
    copies = []
    for k in range(1, n):
        copies.append(pltpu.make_async_remote_copy(
            src_ref=slots.at[me], dst_ref=slots.at[me], send_sem=send.at[k], recv_sem=recv.at[k],
            device_id={axis: lax.rem(me + k, n)}, device_id_type=MESH))
    for copy in copies:
        copy.start()
    return copies


def one_hot(hits):
    return hits.astype(jnp.float32).astype(jnp.bfloat16)


def iota(shape, dim):
    return lax.broadcasted_iota(jnp.int32, shape, dim)


def turn(rows, cols):
    count = rows * cols
    out = lax.broadcasted_iota(jnp.int32, (count, count), 0)
    src = lax.broadcasted_iota(jnp.int32, (count, count), 1)
    return (lax.rem(out, rows) * cols + lax.div(out, rows) == src).astype(jnp.float32).astype(jnp.bfloat16)


def turn_back(rows, cols):
    count = rows * cols
    out = lax.broadcasted_iota(jnp.int32, (count, count), 0)
    src = lax.broadcasted_iota(jnp.int32, (count, count), 1)
    return (lax.rem(out, cols) * rows + lax.div(out, cols) == src).astype(jnp.float32).astype(jnp.bfloat16)


def dot(a, b):
    return jnp.dot(a, b, preferred_element_type=jnp.float32)


def rim_picks(rows, cols):
    shape = (8 * cols, rows * cols)
    out, src = iota(shape, 0), iota(shape, 1)
    d, k = lax.div(out, cols), lax.rem(out, cols)
    last = (rows - 1) * cols
    token = jnp.where(d == 0, k, last + k)
    token = jnp.where(d == 2, k * cols, token)
    token = jnp.where(d == 3, k * cols + cols - 1, token)
    token = jnp.where(d == 4, 0, token)
    token = jnp.where(d == 5, cols - 1, token)
    token = jnp.where(d == 6, last, token)
    token = jnp.where(d == 7, rows * cols - 1, token)
    return one_hot(token == src)


def head_picks(columns, rank, state):
    shape = (columns, 256)
    src, out = iota(shape, 0), iota(shape, 1)
    wide = rank + 2 * state
    part, m = lax.div(out, 128), lax.rem(out, 128)
    base = 2 * part * wide
    at = jnp.where(m < 2 * state, base + rank + m, base + wide + rank + m - 2 * state)
    at = jnp.where(m >= 4 * state, base + m - 4 * state, at)
    at = jnp.where(m >= 4 * state + rank, base + wide + m - 4 * state - rank, at)
    at = jnp.where(m >= 4 * state + 2 * rank, -1, at)
    return one_hot(at == src)


def tissue_column(tissue, rows, cols):
    count = rows * cols
    up = one_hot(lax.div(iota((count, rows), 0), cols) == iota((count, rows), 1))
    spread_out = dot(up, tissue[...].astype(jnp.float32).astype(jnp.bfloat16))
    mine = lax.rem(iota((count, cols), 0), cols) == iota((count, cols), 1)
    return jnp.sum(jnp.where(mine, spread_out, 0.0), axis=1, keepdims=True)


def front(dims, rim_copies, patches, rim_in, w_in, w_conv, bias, w_x, tissue,
          msg_row, msg_col, act_out, gate_out, frame):
    rows, cols, inner, nr, nc, rank, state = dims
    tokens = rows * cols
    projected = dot(patches[...], w_in[...])
    gate_out[...] = projected[:, inner:].astype(jnp.bfloat16)
    body = projected[:, :inner].astype(jnp.bfloat16).astype(jnp.float32)
    frame[1:rows + 1, 1:cols + 1, :] = body.reshape(rows, cols, inner)
    finish(rim_copies)
    rim = dot(rim_in[...].reshape(8 * cols, -1), w_in[:, :inner])
    rim = rim.astype(jnp.bfloat16).astype(jnp.float32)
    r, c = lax.axis_index("row"), lax.axis_index("col")
    pieces = []
    for d, (dr, dc) in enumerate(AROUND):
        inside = (r - dr >= 0) & (r - dr < nr) & (c - dc >= 0) & (c - dc < nc)
        pieces.append(rim[d * cols:(d + 1) * cols] * jnp.where(inside, 1.0, 0.0))
    frame[rows + 1, 1:cols + 1, :] = pieces[0]
    frame[0, 1:cols + 1, :] = pieces[1]
    for i in range(rows):
        frame[i + 1, cols + 1:cols + 2, :] = pieces[2][i:i + 1]
        frame[i + 1, 0:1, :] = pieces[3][i:i + 1]
    frame[rows + 1, cols + 1:cols + 2, :] = pieces[4][0:1]
    frame[rows + 1, 0:1, :] = pieces[5][0:1]
    frame[0, cols + 1:cols + 2, :] = pieces[6][0:1]
    frame[0, 0:1, :] = pieces[7][0:1]
    total = jnp.zeros((rows, cols, inner), jnp.float32) + bias[...].reshape(1, inner)
    for i in range(3):
        for j in range(3):
            total = total + frame[i:i + rows, j:j + cols, :] * w_conv[i, j:j + 1, :]
    act = (total * jax.nn.sigmoid(total)).astype(jnp.bfloat16).reshape(tokens, inner)
    act_out[...] = act
    head = lax.dot_general(act, w_x[...], (((1,), (1,)), ((), ())),
                           preferred_element_type=jnp.float32).astype(jnp.bfloat16)
    head = dot(head, head_picks(w_x.shape[0], rank, state))
    mark = tissue_column(tissue, rows, cols)
    place = lax.rem(iota((tokens, 256), 1), 128)
    head = jnp.where(place == 4 * state + 2 * rank, mark, head).astype(jnp.bfloat16)
    flip = turn(rows, cols)
    head_row = dot(flip, head[:, :128]).astype(jnp.bfloat16)
    act_row = dot(flip, act).astype(jnp.bfloat16)
    for msg, n, top, values in ((msg_row, nc, head_row, act_row), (msg_col, nr, head[:, 128:], act)):
        each = inner // n
        for g in range(n):
            msg[g, :, 0:128] = top
            msg[g, :, 128:128 + each] = values[:, g * each:(g + 1) * each]


def pick_exact(values, picks):
    high = values.astype(jnp.bfloat16)
    rest = values - high.astype(jnp.float32)
    middle = rest.astype(jnp.bfloat16)
    low = (rest - middle.astype(jnp.float32)).astype(jnp.bfloat16)
    return dot(high, picks) + dot(middle, picks) + dot(low, picks)


def gather_weights(first, place, each, width, rank, state, dt_weight, dt_bias, decay,
                   wd_s, bias_s, nd_s, ndb_s):
    inner = dt_weight.shape[2]
    shape = (inner, width)
    picks = one_hot((iota(shape, 0) == iota(shape, 1) + place * each) & (iota(shape, 1) < each))
    top = 4 * state
    for b in range(2):
        here = slice(b * width, (b + 1) * width)
        w = dot(dt_weight[first + b], picks)
        above = top + b * rank
        w = jnp.concatenate([jnp.zeros((above, width), jnp.float32), w,
                             jnp.zeros((128 - above - rank, width), jnp.float32)], axis=0)
        wd_s[:, here] = w.astype(jnp.bfloat16)
        bias = jnp.broadcast_to(dt_bias[first + b:first + b + 1, :], (8, inner))
        bias_s[:, here] = pick_exact(bias, picks)
        rate = pick_exact(decay[first + b], picks) * -LOG2E
        nd_s[:, here] = rate
        for s in range(state):
            ndb_s[s, :, here] = jnp.broadcast_to(rate[s:s + 1], (8, width))


def full(rate, chains):
    return rate if chains == 8 else jnp.concatenate([rate] * (chains // 8), axis=0)


def chain_pass(spec, refs, backward, states, outputs):
    chains, steps, width, state = spec
    dt_ref, du_ref, bc_ref, ndb_ref, y_ref = refs
    b_at = 2 * state if backward else 0
    c_at = b_at + state
    col = width if backward else 0

    def one(i, carry):
        held, total = carry
        t = steps - 1 - i if backward else i
        here = pl.ds(pl.multiple_of(t * chains, chains), chains)
        dt = dt_ref[here, col:col + width]
        du = du_ref[here, col:col + width]
        bc = bc_ref[here, :]
        y = y_ref[here, :] if outputs and backward else None
        fresh = []
        for s in range(state):
            rate = full(ndb_ref[s, :, col:col + width], chains)
            h = jnp.exp2(rate * dt) * held[s] + du * bc[:, b_at + s:b_at + s + 1]
            fresh.append(h)
            if outputs:
                term = h * bc[:, c_at + s:c_at + s + 1]
                y = term if y is None else y + term
        if outputs:
            y_ref[here, :] = y
        return tuple(fresh), total if outputs else total + dt

    start = 0 if outputs else jnp.zeros((chains, width), jnp.float32)
    return lax.fori_loop(0, steps, one, (tuple(states), start), unroll=16)


def shifted(values, by, backward):
    edge = jnp.zeros((by, values.shape[1]), jnp.float32)
    if backward:
        return jnp.concatenate([values[by:], edge], axis=0)
    return jnp.concatenate([edge, values[:-by]], axis=0)


def first_pass(spec, n, me, got, wd_s, bias_s, nd_s, ndb_s, dt_s, du_s, bc_s, y_s, entry_s, sum_s, slots):
    chains, steps, width, each, rank, state = spec
    senders, block = got.shape[0], got.shape[1]
    mark_at = 4 * state + 2 * rank
    for g in range(senders):
        here = slice(g * block, (g + 1) * block)
        head = got[g, :, 0:128]
        wide = head.astype(jnp.float32)
        bc_s[here, :] = wide
        x = dot(head, wd_s[...]) + bias_s[0:1, :]
        dt = (jnp.maximum(x, 0.0) + jnp.log1p(jnp.exp(-jnp.abs(x)))) * wide[:, mark_at:mark_at + 1]
        dt_s[here, :] = dt
        act = got[g, :, 128:128 + width].astype(jnp.float32)
        if each < width:
            act = jnp.where(iota((block, width), 1) < each, act, 0.0)
        du_s[here, 0:width] = dt[:, 0:width] * act
        du_s[here, width:2 * width] = dt[:, width:2 * width] * act
    for b in range(2):
        col = b * width
        zero = [jnp.zeros((chains, width), jnp.float32)] * state
        ends, total = chain_pass((chains, steps, width, state),
                                 (dt_s, du_s, bc_s, ndb_s, y_s), b == 1, zero, False)
        rates = [full(ndb_s[s, :, col:col + width], chains) for s in range(state)]
        by = 1
        while by < chains:
            ends = [jnp.exp2(rate * total) * shifted(end, by, b == 1) + end
                    for rate, end in zip(rates, ends)]
            total = total + shifted(total, by, b == 1)
            by *= 2
        last = 0 if b else chains - 1
        for s in range(state):
            slots[me, b, s:s + 1, :] = ends[s][last:last + 1]
            entry_s[b, s] = shifted(ends[s], 1, b == 1)
        slots[me, b, state:state + 8, :] = jnp.broadcast_to(total[last:last + 1], (8, width))
        sum_s[b] = shifted(total, 1, b == 1)


def second_pass(spec, n, me, nd_s, ndb_s, dt_s, du_s, bc_s, y_s, entry_s, sum_s, slots, y_out):
    chains, steps, width, each, rank, state = spec
    for b in range(2):
        col = b * width
        nd = nd_s[:, col:col + width]
        held = jnp.zeros((state, width), jnp.float32)
        for q in (range(n - 1, -1, -1) if b else range(n)):
            ahead = (q > me) if b else (q < me)
            keep = jnp.where(ahead, 1.0, 0.0)
            after = jnp.exp2(nd * slots[q, b, state:state + 1, :]) * held + slots[q, b, 0:state, :]
            held = held + keep * (after - held)
        start = [
            jnp.exp2(full(ndb_s[s, :, col:col + width], chains) * sum_s[b]) * held[s:s + 1]
            + entry_s[b, s] for s in range(state)]
        chain_pass((chains, steps, width, state),
                   (dt_s, du_s, bc_s, ndb_s, y_s), b == 1, start, True)
    groups, count = y_out.shape[0], y_out.shape[1]
    for g in range(groups):
        y_out[g] = y_s[g * count:(g + 1) * count, :].astype(jnp.bfloat16)


def kernel(dims, specs, patches, tissue, w_in, w_conv, bias, skip, gain, w_x, dt_weight, dt_bias, decay,
           w_out, out, picked, rim_in, frame, act, gate, mixed, rim_send, rim_recv, *scratch):
    rows, cols, inner, nr, nc, rank, state = dims
    r, c = lax.axis_index("row"), lax.axis_index("col")
    near = [(lax.rem(r + dr + nr, nr), lax.rem(c + dc + nc, nc)) for dr, dc in AROUND]
    peers = near[4:]
    peers += [(lax.rem(r + k, nr), c) for k in range(1, nr)]
    peers += [(r, lax.rem(c + k, nc)) for k in range(1, nc)]
    picked[...] = dot(rim_picks(rows, cols), patches[...]).astype(jnp.bfloat16).reshape(picked.shape)
    greet(peers)
    rim_copies = []
    for d, peer in enumerate(near):
        rim_copies.append(pltpu.make_async_remote_copy(
            src_ref=picked.at[d], dst_ref=rim_in.at[d], send_sem=rim_send.at[d],
            recv_sem=rim_recv.at[d], device_id=peer, device_id_type=MESH))
        rim_copies[-1].start()
    half = len(scratch) // 2
    row, col = scratch[:half], scratch[half:]
    parts = ((row, "col", nc, c, "row", nr, r, specs[0], 0), (col, "row", nr, r, "col", nc, c, specs[1], 2))
    front(dims, rim_copies, patches, rim_in, w_in, w_conv, bias, w_x, tissue,
          row[0], col[0], act, gate, frame)
    away = [swap(axis, n, work[0], work[1], *work[4:7]) for work, axis, n, *unused in parts]
    for work, axis, n, me, chain, m, place, spec, first in parts:
        gather_weights(first, me, spec[3], spec[2], rank, state, dt_weight, dt_bias, decay, *work[13:17])
    sums = []
    for p, (work, axis, n, me, chain, m, place, spec, first) in enumerate(parts):
        finish(away[p])
        first_pass(spec, m, place, work[1], *work[13:23], work[23])
        sums.append(spread(chain, m, work[23], work[10], work[11]))
    home = []
    for p, (work, axis, n, me, chain, m, place, spec, first) in enumerate(parts):
        finish(sums[p])
        second_pass(spec, m, place, *work[15:24], work[2])
        home.append(swap(axis, n, work[2], work[3], *work[7:10]))
    finish(home[0])
    flip = turn_back(rows, cols)
    each = inner // nc
    for g in range(nc):
        mixed[:, g * each:(g + 1) * each] = dot(flip, row[3][g])[:, :each]
    finish(home[1])
    each = inner // nr
    for g in range(nr):
        here = slice(g * each, (g + 1) * each)
        mixed[:, here] = mixed[:, here] + col[3][g].astype(jnp.float32)[:, :each]
    total = mixed[...] + skip[...].reshape(1, inner) * act[...].astype(jnp.float32)
    centered = total - jnp.mean(total, axis=1, keepdims=True)
    variance = jnp.mean(centered * centered, axis=1, keepdims=True)
    normed = centered * lax.rsqrt(variance + 1e-05) * gain[...].reshape(1, inner)
    gate_wide = gate[...].astype(jnp.float32)
    value = (normed * (gate_wide * jax.nn.sigmoid(gate_wide))).astype(jnp.bfloat16)
    result = dot(value, w_out[...]) * tissue_column(tissue, rows, cols)
    out[...] = result


def per_device(nr, nc, patches, tissue, in_weight, conv_weight, conv_bias, x_weight, dt_weight,
               dt_bias, decay_rate, skip_gain, norm_gain, out_weight):
    rows, cols, channels = patches.shape
    tokens = rows * cols
    inner = out_weight.shape[0]
    state = decay_rate.shape[2]
    rank = dt_weight.shape[1]
    bf, f32 = jnp.bfloat16, jnp.float32
    dma = pltpu.SemaphoreType.DMA
    dims = (rows, cols, inner, nr, nc, rank, state)
    specs, scratch = [], [
        pltpu.VMEM((8, cols, channels), bf), pltpu.VMEM((8, cols, channels), bf),
        pltpu.VMEM((rows + 2, -(-(cols + 2) // 8) * 8, inner), f32),
        pltpu.VMEM((tokens, inner), bf), pltpu.VMEM((tokens, inner), bf),
        pltpu.VMEM((tokens, inner), f32), dma((8,)), dma((8,))]
    for chains, n, m, length in ((rows, nc, nr, cols), (cols, nr, nc, rows)):
        each = inner // n
        width = lanes(each)
        steps = n * length
        specs.append((chains, steps, width, each, rank, state))
        count = chains * steps
        scratch += [
            pltpu.VMEM((n, tokens, 128 + width), bf), pltpu.VMEM((n, tokens, 128 + width), bf),
            pltpu.VMEM((n, tokens, width), bf), pltpu.VMEM((n, tokens, width), bf),
            dma((n,)), dma((n,)), dma((1,)), dma((n,)), dma((n,)), dma((1,)), dma((m,)), dma((m,)),
            dma((1,)),
            pltpu.VMEM((128, 2 * width), bf), pltpu.VMEM((8, 2 * width), f32),
            pltpu.VMEM((state, 2 * width), f32), pltpu.VMEM((state, 8, 2 * width), f32),
            pltpu.VMEM((count, 2 * width), f32), pltpu.VMEM((count, 2 * width), f32),
            pltpu.VMEM((count, 128), f32), pltpu.VMEM((count, width), f32),
            pltpu.VMEM((2, state, chains, width), f32), pltpu.VMEM((2, chains, width), f32),
            pltpu.VMEM((m, 2, state + 8, width), f32)]
    out = pl.pallas_call(
        functools.partial(kernel, dims, specs),
        out_shape=jax.ShapeDtypeStruct((tokens, channels), f32),
        in_specs=[VMEM] * 12, out_specs=VMEM, scratch_shapes=scratch,
        compiler_params=pltpu.CompilerParams(
            collective_id=0, has_side_effects=True, vmem_limit_bytes=LIMIT),
        name="block",
    )(patches.reshape(tokens, channels), tissue, in_weight, conv_weight, conv_bias, skip_gain, norm_gain, x_weight.T,
      dt_weight, dt_bias, jnp.transpose(decay_rate, (0, 2, 1)), out_weight)
    return out.astype(bf).reshape(rows, cols, channels)


def solution(mesh):
    grid = P("row", "col")
    return jax.shard_map(
        functools.partial(per_device, mesh.shape["row"], mesh.shape["col"]), mesh=mesh,
        in_specs=(P("row", "col", None), grid) + (P(),) * 10,
        out_specs=P("row", "col", None), check_vma=False)
```
